128 devices in a mesh: user: 32 (over y, x, core), item: 4 (over z).
Axes of the slice: x: 4, y: 4, z: 4, core: 2. Of those that a mesh axis runs over, the one named last changes fastest.
Arguments:
- user_emb: bfloat16 [32, 1024, 256], P('user'), may hold values from -6 to 6
- item_emb: bfloat16 [32, 4, 128, 256], P('user', 'item'), may hold values from -6 to 6
- user_degree: int32 [32, 1024], P('user'), may hold values from 16 to 160
- item_degree: int32 [32, 4, 128], P('user', 'item'), may hold values from 16 to 160
- tiles: int32 [32, 4, 64, 128, 128], P('user', 'item'), may hold values 0 or 1
- tile_user: int32 [32, 4, 64], P('user', 'item'), may hold values from 0 to 7
- tile_item: int32 [32, 4, 64], P('user', 'item'), may hold values from 0 to 31
- tile_count: int32 [32, 4], P('user', 'item'), may hold values from 8 to 64, as said below
- triple_user: int32 [32, 4, 256], P('user', 'item'), may hold values from 0 to 1023
- triple_pos: int32 [32, 4, 256], P('user', 'item'), may hold values from 0 to 4095
- triple_neg: int32 [32, 4, 256], P('user', 'item'), may hold values from 0 to 4095
Outputs:
- grad_user: float32 [32, 1024, 256], P('user')
- grad_item: float32 [32, 4, 128, 256], P('user', 'item')
The draws below stay inside these ranges and needn't reach their ends.
Inputs may be any that keep to these rules, and one draw needn't show every extreme that they name: Slots 0 to tile_count[a, c] - 1 of tiles[a, c] are live, the others are not part of R; in every draw some device has all 64 slots live.
All inputs are finite; a program needn't handle non-finite values. No bound on the sum of `tiles` on one device may be relied on, other than what follows from the above.
Results may differ from the reference program's by a relative error of at most 0.006.
Values may be sent and summed in bfloat16 or wider, within the bound.
A program may use at most 128 MiB of HBM per device.

```python
import math
import jax
import jax.numpy as jnp
import numpy as np
from jax import lax

D = 256
BLOCK = 128
LAYERS = 2
UB_DEV = 8
TILES_DEV = 64
TRIP_DEV = 256
ROWS_U = 1024
ROWS_I = 128
COL_BLOCKS = 32
COL_ROWS = 4096
N_USER = 32
N_ITEM = 4


def draw_tile_count(key, part):
    key = jax.random.fold_in(key, 7)
    first, second, third = jax.random.split(key, 3)
    base = jax.random.randint(first, (N_USER, N_ITEM), TILES_DEV // 8, TILES_DEV // 2 + 1)
    heavy = jax.random.randint(second, (N_USER, N_ITEM), 0, 8) == 0
    counts = jnp.where(heavy, TILES_DEV, base).reshape(-1)
    chosen = jax.random.randint(third, (), 0, N_USER * N_ITEM)
    counts = jnp.where(jnp.arange(N_USER * N_ITEM) == chosen, TILES_DEV, counts)
    return counts.reshape(N_USER, N_ITEM).astype(jnp.int32)


def with_ends(values, own_key, smallest, high):
    spot = [jax.random.randint(jax.random.fold_in(own_key, axis), (), 0, length) for axis, length in enumerate(values.shape)]
    main_axis = values.shape.index(max(values.shape))
    neighbour = spot[:main_axis] + [(spot[main_axis] + 1) % values.shape[main_axis]] + spot[main_axis + 1:]
    return values.at[tuple(spot)].set(smallest).at[tuple(neighbour)].set(high)


def block_scale(own_key, extent, cuts, low, high):
    def one(position, blocks):
        draws = jax.random.uniform(jax.random.fold_in(jax.random.fold_in(own_key, 6), position), (blocks,), jnp.float32, low / len(cuts), high / len(cuts))
        return jnp.repeat(jnp.exp(draws), extent[position] // blocks).reshape((-1,) + (1,) * (len(extent) - position - 1))

    factor_of = one(*cuts[0])
    for cut in cuts[1:]:
        factor_of = factor_of * one(*cut)
    return factor_of


def rank_bounds(amount, lean):
    portions = [(1 << 20) // math.isqrt(grade ** lean) + 1 for grade in range(1, amount + 1)]
    width = 1 + sum(portions) // (1 << 30)
    return np.cumsum(np.array([max(1, weight // width) for weight in portions]))


def ranked(own_key, shape, number_of, lean):
    grid = rank_bounds(number_of, lean)
    pick = jax.random.randint(jax.random.fold_in(own_key, 1), shape, 0, int(grid[number_of - 1]))
    rank = jnp.searchsorted(jnp.asarray(grid, jnp.int32), pick, side="right")
    return jax.random.permutation(jax.random.fold_in(own_key, 2), number_of)[rank].astype(jnp.int32)


def bell_draw(own_key, extent, spread, reach, cuts=(), kind=jnp.bfloat16):
    drawn = spread * jax.random.normal(own_key, extent, jnp.float32)
    if cuts:
        drawn = drawn * block_scale(own_key, extent, cuts, -0.22, 0.18)
    return jnp.clip(drawn, -reach, reach).astype(kind)


def setup_inputs(seed: int = 0) -> dict:
    key_of = jax.random.split(jax.random.key(seed), 12)
    return {
        "user_emb": bell_draw(key_of[0], (N_USER, ROWS_U, D), 1.0, 6.0, ((0, 32),)),
        "item_emb": bell_draw(key_of[1], (N_USER, N_ITEM, ROWS_I, D), 1.0, 6.0, ((0, 32), (1, 4))),
        "user_degree": with_ends(jax.random.randint(key_of[2], (N_USER, ROWS_U), 16, 161), jax.random.fold_in(key_of[2], 1), 16, 160).astype(jnp.int32),
        "item_degree": with_ends(jax.random.randint(key_of[3], (N_USER, N_ITEM, ROWS_I), 16, 161), jax.random.fold_in(key_of[3], 1), 16, 160).astype(jnp.int32),
        "tiles": with_ends((jax.random.randint(key_of[4], (N_USER, N_ITEM, TILES_DEV, BLOCK, BLOCK), 0, 32) < 1).astype(jnp.int32), jax.random.fold_in(key_of[4], 1), 0, 1),
        "tile_user": with_ends(jax.random.randint(key_of[5], (N_USER, N_ITEM, TILES_DEV), 0, UB_DEV), jax.random.fold_in(key_of[5], 1), 0, UB_DEV - 1).astype(jnp.int32),
        "tile_item": with_ends(ranked(key_of[6], (N_USER, N_ITEM, TILES_DEV), COL_BLOCKS, 2), jax.random.fold_in(key_of[6], 3), 0, COL_BLOCKS - 1).astype(jnp.int32),
        "tile_count": draw_tile_count(jax.random.fold_in(key_of[11], 71), 0),
        "triple_user": with_ends(jax.random.randint(key_of[8], (N_USER, N_ITEM, TRIP_DEV), 0, ROWS_U), jax.random.fold_in(key_of[8], 1), 0, ROWS_U - 1).astype(jnp.int32),
        "triple_pos": with_ends(jax.random.randint(key_of[9], (N_USER, N_ITEM, TRIP_DEV), 0, COL_ROWS), jax.random.fold_in(key_of[9], 1), 0, COL_ROWS - 1).astype(jnp.int32),
        "triple_neg": with_ends(jax.random.randint(key_of[10], (N_USER, N_ITEM, TRIP_DEV), 0, COL_ROWS), jax.random.fold_in(key_of[10], 1), 0, COL_ROWS - 1).astype(jnp.int32),
    }


def device_terms(mats, rows_pick, cols_pick, feed_col, feed_user):
    high = lax.Precision.HIGHEST
    blocks_col = feed_col.reshape(COL_BLOCKS, BLOCK, D)[cols_pick].astype(jnp.float32)
    user_prods = jnp.einsum('tuv,tvd->tud', mats, blocks_col, precision=high)
    user_part = jax.ops.segment_sum(user_prods, rows_pick, num_segments=UB_DEV).reshape(ROWS_U, D)
    blocks_user = feed_user.reshape(UB_DEV, BLOCK, D)[rows_pick].astype(jnp.float32)
    item_prods = jnp.einsum('tuv,tud->tvd', mats, blocks_user, precision=high)
    item_part = jax.ops.segment_sum(item_prods, cols_pick, num_segments=COL_BLOCKS).reshape(COL_ROWS, D)
    return (user_part, item_part)

def propagate(feed_user, feed_item, flat_tiles, live, rows, cols):

    def step(carry, index):
        users, items = carry
        owner = index // N_ITEM
        column = index % N_ITEM
        mats = lax.dynamic_index_in_dim(flat_tiles, index, 0, keepdims=False).astype(jnp.float32)
        mats = mats * lax.dynamic_index_in_dim(live, index, 0, keepdims=False)[:, None, None]
        rows_pick = lax.dynamic_index_in_dim(rows, index, 0, keepdims=False)
        cols_pick = lax.dynamic_index_in_dim(cols, index, 0, keepdims=False)
        feed_col = lax.dynamic_index_in_dim(feed_item, column, 1, keepdims=False).reshape(COL_ROWS, D)
        feed_own = lax.dynamic_index_in_dim(feed_user, owner, 0, keepdims=False)
        user_part, item_part = device_terms(mats, rows_pick, cols_pick, feed_col, feed_own)
        users = users.at[owner].add(user_part)
        items = items.at[:, column].add(item_part.reshape(N_USER, ROWS_I, D))
        return ((users, items), None)
    start = (jnp.zeros((N_USER, ROWS_U, D), jnp.float32), jnp.zeros((N_USER, N_ITEM, ROWS_I, D), jnp.float32))
    indices = jnp.arange(N_USER * N_ITEM, dtype=jnp.int32)
    (users, items), unused = lax.scan(step, start, indices)
    return (users, items)

def reference(user_emb, item_emb, user_degree, item_degree, tiles, tile_user, tile_item, tile_count, triple_user, triple_pos, triple_neg):
    devices = N_USER * N_ITEM
    flat_tiles = tiles.reshape(devices, TILES_DEV, BLOCK, BLOCK)
    live = (jnp.arange(TILES_DEV, dtype=jnp.int32)[None, :] < tile_count.reshape(devices, 1)).astype(jnp.float32)
    rows = tile_user.reshape(devices, TILES_DEV)
    cols = tile_item.reshape(devices, TILES_DEV)
    user_scale = lax.rsqrt(user_degree.astype(jnp.float32))[..., None]
    item_scale = lax.rsqrt(item_degree.astype(jnp.float32))[..., None]

    def apply(feed_user, feed_item):
        return propagate(feed_user, feed_item, flat_tiles, live, rows, cols)
    user_state, item_state = (user_emb, item_emb)
    user_total = user_state.astype(jnp.float32)
    item_total = item_state.astype(jnp.float32)
    for layer in range(LAYERS):
        feed_user = (user_scale * user_state.astype(jnp.float32)).astype(jnp.bfloat16)
        feed_item = (item_scale * item_state.astype(jnp.float32)).astype(jnp.bfloat16)
        user_sum, item_sum = apply(feed_user, feed_item)
        user_state = (user_scale * user_sum).astype(jnp.bfloat16)
        item_state = (item_scale * item_sum).astype(jnp.bfloat16)
        user_total = user_total + user_state.astype(jnp.float32)
        item_total = item_total + item_state.astype(jnp.float32)
    final_user = (user_total / (LAYERS + 1.0)).astype(jnp.bfloat16)
    final_item = (item_total / (LAYERS + 1.0)).astype(jnp.bfloat16)
    shard_index = jnp.arange(N_USER, dtype=jnp.int32)[:, None, None]
    column_index = jnp.arange(N_ITEM, dtype=jnp.int32)[None, :, None]
    user_rows = final_user[shard_index, triple_user].astype(jnp.float32)
    pos_owner = triple_pos // ROWS_I
    pos_local = triple_pos % ROWS_I
    neg_owner = triple_neg // ROWS_I
    neg_local = triple_neg % ROWS_I
    diff = final_item[pos_owner, column_index, pos_local].astype(jnp.float32) - final_item[neg_owner, column_index, neg_local].astype(jnp.float32)
    score = lax.optimization_barrier(jnp.sum(user_rows * diff, axis=-1))
    weight = jax.nn.sigmoid(-score)[..., None]
    grad_u = jnp.zeros((N_USER, ROWS_U, D), jnp.float32).at[shard_index, triple_user].add(-weight * diff)
    grad_i = jnp.zeros((N_USER, N_ITEM, ROWS_I, D), jnp.float32)
    grad_i = grad_i.at[pos_owner, column_index, pos_local].add(-weight * user_rows)
    grad_i = grad_i.at[neg_owner, column_index, neg_local].add(weight * user_rows)
    carry_user, carry_item = (grad_u, grad_i)
    for layer in range(LAYERS):
        feed_user = (user_scale * carry_user).astype(jnp.bfloat16)
        feed_item = (item_scale * carry_item).astype(jnp.bfloat16)
        user_sum, item_sum = apply(feed_user, feed_item)
        carry_user = grad_u + user_scale * user_sum
        carry_item = grad_i + item_scale * item_sum
    return (carry_user / (LAYERS + 1.0), carry_item / (LAYERS + 1.0))
```

```python
import functools

import jax
import jax.numpy as jnp
from jax import lax
from jax.experimental import pallas as pl
from jax.experimental.pallas import tpu as pltpu
from jax.sharding import PartitionSpec as P

F32 = jnp.float32
BF16 = jnp.bfloat16
MESH = pl.DeviceIdType.MESH
SIDE = 4
BLOCK = 128
CHUNK = SIDE * BLOCK


def build_kernel(count_ref, rows_ref, cols_ref, tiles_ref, r_ref, rt_ref):
    zero_rows = 256

    def clear(i, carry):
        at = pl.ds(pl.multiple_of(i * zero_rows, zero_rows), zero_rows)
        r_ref[at, :] = jnp.zeros((zero_rows, r_ref.shape[1]), BF16)
        for j in range(4):
            at = pl.ds(pl.multiple_of((i * 4 + j) * zero_rows, zero_rows), zero_rows)
            rt_ref[at, :] = jnp.zeros((zero_rows, rt_ref.shape[1]), BF16)
        return carry

    lax.fori_loop(0, r_ref.shape[0] // zero_rows, clear, 0)

    def add(slot, carry):
        users = pl.ds(pl.multiple_of(rows_ref[slot] * BLOCK, BLOCK), BLOCK)
        items = pl.ds(pl.multiple_of(cols_ref[slot] * BLOCK, BLOCK), BLOCK)
        tile = tiles_ref[slot].astype(F32)
        r_ref[users, items] = (r_ref[users, items].astype(F32) + tile).astype(BF16)
        rt_ref[items, users] = (rt_ref[items, users].astype(F32) + tile.T).astype(BF16)
        return carry

    lax.fori_loop(0, count_ref[0], add, 0)


def build(count, rows, cols, tiles, users, items):
    smem = pl.BlockSpec(memory_space=pltpu.SMEM)
    vmem = pl.BlockSpec(memory_space=pltpu.VMEM)
    return pl.pallas_call(
        build_kernel,
        out_shape=(
            jax.ShapeDtypeStruct((users, items), BF16),
            jax.ShapeDtypeStruct((items, users), BF16),
        ),
        in_specs=[smem, smem, smem, vmem],
        out_specs=(vmem, vmem),
        compiler_params=pltpu.CompilerParams(vmem_limit_bytes=40 * 2**20),
        name="build",
    )(count, rows, cols, tiles)


def main_kernel(
    user_emb, item_emb, ru, ri, tu_col, tp_col, tn_col, tu_row, tp_row, tn_row, r_hbm, rt_hbm,
    out_user, out_item,
    r_mat, rt_mat, feeds, users, sib_in, sib_out, q_out, q_half, q_full, p_out, p_half, p_full,
    z_out, z_half, z_full, part, upart, user_total, item_total, user_base, item_base, values,
    load_sem, ag_recv, ag_send, rs_recv, rs_send, z_recv, z_send,
):
    a = lax.axis_index("user")
    z = lax.axis_index("item")
    core = a % 2
    x = (a // 2) % SIDE
    y = a // (2 * SIDE)
    p = x + core * (y - x)
    q = y + core * (x - y)
    sibling = a + 1 - 2 * core
    rows_u = user_emb.shape[0]
    quarter = rows_u // SIDE
    half_q = quarter // 2

    def at_pq(pp, qq):
        yy = qq + core * (pp - qq)
        xx = pp + core * (qq - pp)
        return {"user": (yy * SIDE + xx) * 2 + core}

    def turn(i, by):
        return (i + by) % SIDE

    to_p = {1: at_pq(turn(p, 1), q), -1: at_pq(turn(p, 3), q)}
    to_q = {1: at_pq(p, turn(q, 1)), -1: at_pq(p, turn(q, 3))}
    to_z = {1: {"item": turn(z, 1)}, -1: {"item": turn(z, 3)}}
    to_s = {"user": sibling}

    def rows(start, count):
        return pl.ds(pl.multiple_of(start, 64), count)

    def copy(src, dst, send, recv, device):
        return pltpu.make_async_remote_copy(
            src_ref=src, dst_ref=dst, send_sem=send, recv_sem=recv,
            device_id=device, device_id_type=MESH,
        )

    loads = (
        pltpu.make_async_copy(rt_hbm, rt_mat, load_sem.at[0]),
        pltpu.make_async_copy(r_hbm, r_mat, load_sem.at[1]),
    )
    for load in loads:
        load.start()

    barrier = pltpu.get_barrier_semaphore()
    partners = (to_p[1], to_p[-1], to_q[1], to_q[-1], to_z[1], to_z[-1], to_s)
    for device in partners:
        pl.semaphore_signal(barrier, inc=1, device_id=device, device_id_type=MESH)

    def slot(qq, pp, extra=0):
        return ((core * SIDE + qq) * SIDE + pp) * BLOCK + extra

    def gather_copy(r, start, count, device, recv):
        ref = feeds.at[r, rows(start, count)]
        return copy(ref, ref, ag_send.at[r], ag_recv.at[r, recv], device)

    def to_sibling(r, qq, pp):
        gather_copy(r, slot(qq, pp), BLOCK, to_s, 16 + qq).start()

    def spread_block(r, rel):
        pp = turn(p, rel)
        gather_copy(r, slot(q, pp), BLOCK, to_q[1], 4 + rel).start()
        gather_copy(r, slot(q, pp), BLOCK, to_q[-1], 8 + rel).start()
        to_sibling(r, q, pp)

    def gather_start(r):
        gather_copy(r, slot(q, p), BLOCK, to_p[1], 0).start()
        gather_copy(r, slot(q, p), BLOCK, to_p[-1], 1).start()
        spread_block(r, 0)

    def gather_p(r):
        before, after, far = turn(p, 3), turn(p, 1), turn(p, 2)
        gather_copy(r, slot(q, before), BLOCK, to_p[1], 0).wait_recv()
        gather_copy(r, slot(q, before), BLOCK // 2, to_p[1], 2).start()
        spread_block(r, 3)
        gather_copy(r, slot(q, after), BLOCK, to_p[-1], 1).wait_recv()
        gather_copy(r, slot(q, after, BLOCK // 2), BLOCK // 2, to_p[-1], 3).start()
        spread_block(r, 1)

    def gather_far(r):
        far = turn(p, 2)
        gather_copy(r, slot(q, far), BLOCK // 2, to_p[1], 2).wait_recv()
        gather_copy(r, slot(q, far, BLOCK // 2), BLOCK // 2, to_p[-1], 3).wait_recv()
        spread_block(r, 2)

    def gather_q(r):
        for rel in (0, 3, 1, 2):
            pp = turn(p, rel)
            qq = turn(q, 3)
            gather_copy(r, slot(qq, pp), BLOCK, to_q[1], 4 + rel).wait_recv()
            if rel in (0, 2):
                gather_copy(r, slot(qq, pp), BLOCK, to_q[1], 12 + rel).start()
            to_sibling(r, qq, pp)
            qq = turn(q, 1)
            gather_copy(r, slot(qq, pp), BLOCK, to_q[-1], 8 + rel).wait_recv()
            if rel in (1, 3):
                gather_copy(r, slot(qq, pp), BLOCK, to_q[-1], 12 + rel).start()
            to_sibling(r, qq, pp)

    def gather_end(r):
        qq = turn(q, 2)
        for rel in (0, 3, 1, 2):
            pp = turn(p, rel)
            gather_copy(r, slot(qq, pp), BLOCK, to_q[1], 12 + rel).wait_recv()
            to_sibling(r, qq, pp)
        for other in range(SIDE):
            start = ((1 - core) * SIDE + other) * CHUNK
            gather_copy(r, start, CHUNK, to_s, 16 + other).wait_recv()

    def gather_sent(r):
        gather_copy(r, 0, 31 * BLOCK, to_s, 0).wait_send()

    def make_chunk(term, chunk, out_ref):
        def step(i, carry):
            out_ref[rows(i * BLOCK, BLOCK), :] = term(chunk, i).astype(out_ref.dtype)
            return carry

        lax.fori_loop(0, SIDE, step, 0)

    def sum_sibling(r, term):
        def step(j, carry):
            theirs = turn(p, 2 - j + 3 * (j // 2) - 2 * (j // 3))
            make_chunk(term, (1 - core) * SIDE + theirs, sib_out.at[theirs])
            copy(
                sib_out.at[theirs], sib_in.at[r, theirs], rs_send.at[r, 0],
                rs_recv.at[r, theirs], to_s,
            ).start()
            return carry

        lax.fori_loop(0, SIDE, step, 0)

    def own_chunk(r, term, qq):
        make_chunk(term, core * SIDE + qq, part)
        copy(
            sib_out.at[qq], sib_in.at[r, qq], rs_send.at[r, 0], rs_recv.at[r, qq], to_s
        ).wait_recv()
        return part[...] + sib_in[r, qq].astype(F32)

    def q_copy(r, src, dst, recv, device):
        return copy(src, dst, rs_send.at[r, 1], rs_recv.at[r, recv], device)

    def p_copy(r, src, dst, recv, device):
        return copy(src, dst, rs_send.at[r, 2], rs_recv.at[r, recv], device)

    half_c = CHUNK // 2
    half_b = BLOCK // 2

    def sum_q_far(r, term):
        q_out[0] = own_chunk(r, term, turn(q, 2)).astype(BF16)
        q_copy(r, q_out.at[0, :half_c], q_half.at[r, 0], 4, to_q[1]).start()
        q_copy(r, q_out.at[0, half_c:], q_half.at[r, 1], 5, to_q[-1]).start()

    def sum_q_near(r, term):
        value = own_chunk(r, term, turn(q, 1))
        q_out[1, half_c:, :] = value[half_c:].astype(BF16)
        q_copy(r, q_out.at[0, :half_c], q_half.at[r, 0], 4, to_q[1]).wait_recv()
        q_out[1, :half_c, :] = (value[:half_c] + q_half[r, 0].astype(F32)).astype(BF16)
        q_copy(r, q_out.at[1], q_full.at[r, 0], 6, to_q[1]).start()
        value = own_chunk(r, term, turn(q, 3))
        q_out[2, :half_c, :] = value[:half_c].astype(BF16)
        q_copy(r, q_out.at[0, half_c:], q_half.at[r, 1], 5, to_q[-1]).wait_recv()
        q_out[2, half_c:, :] = (value[half_c:] + q_half[r, 1].astype(F32)).astype(BF16)
        q_copy(r, q_out.at[2], q_full.at[r, 1], 7, to_q[-1]).start()

    def sum_q_end(r, term):
        value = own_chunk(r, term, q)
        q_copy(r, q_out.at[1], q_full.at[r, 0], 6, to_q[1]).wait_recv()
        value = value + q_full[r, 0].astype(F32)
        q_copy(r, q_out.at[2], q_full.at[r, 1], 7, to_q[-1]).wait_recv()
        part[...] = value + q_full[r, 1].astype(F32)
        p_out[0] = part[rows(turn(p, 2) * BLOCK, BLOCK), :].astype(BF16)
        p_copy(r, p_out.at[0, :half_b], p_half.at[r, 0], 8, to_p[1]).start()
        p_copy(r, p_out.at[0, half_b:], p_half.at[r, 1], 9, to_p[-1]).start()

    def sum_p_near(r):
        value = part[rows(turn(p, 1) * BLOCK, BLOCK), :]
        p_copy(r, p_out.at[0, :half_b], p_half.at[r, 0], 8, to_p[1]).wait_recv()
        p_out[1, :half_b, :] = (value[:half_b] + p_half[r, 0].astype(F32)).astype(BF16)
        p_out[1, half_b:, :] = value[half_b:].astype(BF16)
        p_copy(r, p_out.at[1], p_full.at[r, 0], 10, to_p[1]).start()
        value = part[rows(turn(p, 3) * BLOCK, BLOCK), :]
        p_copy(r, p_out.at[0, half_b:], p_half.at[r, 1], 9, to_p[-1]).wait_recv()
        p_out[2, half_b:, :] = (value[half_b:] + p_half[r, 1].astype(F32)).astype(BF16)
        p_out[2, :half_b, :] = value[:half_b].astype(BF16)
        p_copy(r, p_out.at[2], p_full.at[r, 1], 11, to_p[-1]).start()

    def sum_p_end(r):
        p_copy(r, p_out.at[1], p_full.at[r, 0], 10, to_p[1]).wait_recv()
        p_copy(r, p_out.at[2], p_full.at[r, 1], 11, to_p[-1]).wait_recv()
        value = part[rows(p * BLOCK, BLOCK), :]
        return value + p_full[r, 0].astype(F32) + p_full[r, 1].astype(F32)

    def sums_sent(r):
        copy(sib_out, sib_in.at[r], rs_send.at[r, 0], rs_recv.at[r, 0], to_s).wait_send()
        q_copy(r, q_out, q_out, 4, to_q[1]).wait_send()
        p_copy(r, p_out, p_out, 8, to_p[1]).wait_send()

    def z_copy(r, src, dst, recv, device):
        return copy(src, dst, z_send.at[r, 0], z_recv.at[r, recv], device)

    def u_copy(r, start, count, recv, device):
        ref = users.at[r + 1, rows(start, count)]
        return copy(ref, ref, z_send.at[r, 1], z_recv.at[r, recv], device)

    def make_users(term):
        def step(i, carry):
            upart[rows(i * BLOCK, BLOCK), :] = term(i)
            return carry

        lax.fori_loop(0, rows_u // BLOCK, step, 0)

    def user_far(r):
        z_out[0] = upart[rows(turn(z, 2) * quarter, quarter), :].astype(BF16)
        z_copy(r, z_out.at[0, :half_q], z_half.at[r, 0], 0, to_z[1]).start()
        z_copy(r, z_out.at[0, half_q:], z_half.at[r, 1], 1, to_z[-1]).start()

    def user_near(r):
        value = upart[rows(turn(z, 1) * quarter, quarter), :]
        z_copy(r, z_out.at[0, :half_q], z_half.at[r, 0], 0, to_z[1]).wait_recv()
        z_out[1, :half_q, :] = (value[:half_q] + z_half[r, 0].astype(F32)).astype(BF16)
        z_out[1, half_q:, :] = value[half_q:].astype(BF16)
        z_copy(r, z_out.at[1], z_full.at[r, 0], 2, to_z[1]).start()
        value = upart[rows(turn(z, 3) * quarter, quarter), :]
        z_copy(r, z_out.at[0, half_q:], z_half.at[r, 1], 1, to_z[-1]).wait_recv()
        z_out[2, half_q:, :] = (value[half_q:] + z_half[r, 1].astype(F32)).astype(BF16)
        z_out[2, :half_q, :] = value[:half_q].astype(BF16)
        z_copy(r, z_out.at[2], z_full.at[r, 1], 3, to_z[-1]).start()

    def user_end(r):
        z_copy(r, z_out.at[1], z_full.at[r, 0], 2, to_z[1]).wait_recv()
        z_copy(r, z_out.at[2], z_full.at[r, 1], 3, to_z[-1]).wait_recv()
        value = upart[rows(z * quarter, quarter), :]
        return value + z_full[r, 0].astype(F32) + z_full[r, 1].astype(F32)

    def user_spread(r, value):
        users[r + 1, rows(z * quarter, quarter), :] = value
        u_copy(r, z * quarter, quarter, 4, to_z[1]).start()
        u_copy(r, z * quarter, quarter, 5, to_z[-1]).start()

    def user_forward(r):
        before, after = turn(z, 3) * quarter, turn(z, 1) * quarter
        u_copy(r, before, quarter, 4, to_z[1]).wait_recv()
        u_copy(r, before, half_q, 6, to_z[1]).start()
        u_copy(r, after, quarter, 5, to_z[-1]).wait_recv()
        u_copy(r, after + half_q, half_q, 7, to_z[-1]).start()

    def user_ready(r):
        far = turn(z, 2) * quarter
        u_copy(r, far, half_q, 6, to_z[1]).wait_recv()
        u_copy(r, far + half_q, half_q, 7, to_z[-1]).wait_recv()

    def users_sent(r):
        z_copy(r, z_out, z_out, 0, to_z[1]).wait_send()
        u_copy(r, 0, 3 * quarter, 4, to_z[1]).wait_send()

    def item_term(r):
        def term(chunk, i):
            mat = rt_mat[rows(chunk * CHUNK + i * BLOCK, BLOCK), :]
            return jnp.dot(mat, users[r], preferred_element_type=F32)

        return term

    def user_term(r):
        def term(i):
            mat = r_mat[rows(i * BLOCK, BLOCK), :]
            return jnp.dot(mat, feeds[r], preferred_element_type=F32)

        return term

    own_u = rows(z * quarter, quarter)
    own_slot = rows(slot(q, p), BLOCK)

    def exchange(r, items, make_user_parts, user_update, item_update, gathering):
        sum_sibling(r, items)
        if gathering:
            gather_p(r)
        sum_q_far(r, items)
        if gathering:
            gather_far(r)
            gather_q(r)
        sum_q_near(r, items)
        if gathering:
            gather_end(r)
        make_user_parts()
        user_far(r)
        sum_q_end(r, items)
        user_near(r)
        sum_p_near(r)
        user_spread(r, user_update(user_end(r)))
        item_update(sum_p_end(r))
        user_forward(r)
        user_ready(r)
        sums_sent(r)
        users_sent(r)
        gather_sent(r)

    eu = user_emb[...].astype(F32)
    users[0] = (ru[...] * eu).astype(BF16)
    ei = item_emb[...].astype(F32)
    feeds[0, own_slot, :] = (ri[...] * ei).astype(BF16)
    user_total[...] = user_emb[own_u, :].astype(F32)
    item_total[...] = ei
    pl.semaphore_wait(barrier, len(partners))
    gather_start(0)
    loads[0].wait()
    loads[1].wait()

    def forward(r, carry):
        def user_update(value):
            state = (ru[own_u, :] * value).astype(BF16).astype(F32)
            user_total[...] += state
            return jnp.where(r == 0, ru[own_u, :] * state, user_total[...] / 3.0).astype(BF16)

        def item_update(value):
            state = (ri[...] * value).astype(BF16).astype(F32)
            item_total[...] += state
            feeds[r + 1, own_slot, :] = jnp.where(
                r == 0, ri[...] * state, item_total[...] / 3.0
            ).astype(BF16)
            gather_start(r + 1)

        exchange(
            r, item_term(r), lambda: make_users(user_term(r)), user_update, item_update, True
        )
        return carry

    lax.fori_loop(0, 2, forward, 0)

    gather_p(2)
    gather_far(2)
    gather_q(2)
    wide = 2 * BLOCK

    def lanes(i, width):
        return i * width + lax.broadcasted_iota(jnp.int32, (wide, width), 1)

    def pick_user(i, carry):
        hot = (tu_col[...] == lanes(i, BLOCK)).astype(F32).astype(BF16)
        values[0] += jnp.dot(hot, users[2, rows(i * BLOCK, BLOCK), :], preferred_element_type=F32)
        return carry

    def pick_item(i, carry):
        spot = lanes(i, BLOCK)
        hot = ((tp_col[...] == spot).astype(F32) - (tn_col[...] == spot).astype(F32)).astype(BF16)
        values[1] += jnp.dot(hot, feeds[2, rows(i * BLOCK, BLOCK), :], preferred_element_type=F32)
        return carry

    values[...] = jnp.zeros_like(values)
    lax.fori_loop(0, rows_u // BLOCK, pick_user, 0)
    gather_end(2)
    lax.fori_loop(0, feeds.shape[1] // BLOCK, pick_item, 0)
    score = jnp.sum(values[0] * values[1], axis=1, keepdims=True)
    weight = jax.nn.sigmoid(-score)
    user_value = -weight * values[1]
    item_value = -weight * values[0]

    def split(value):
        high = value.astype(BF16)
        return high, (value - high.astype(F32)).astype(BF16)

    def spots(start):
        return start + lax.broadcasted_iota(jnp.int32, (BLOCK, wide), 0)

    user_high, user_low = split(user_value)
    item_high, item_low = split(item_value)
    upart_split = (user_high, user_low)
    values_b = (item_high, item_low)

    def grad_item_term(chunk, i):
        spot = spots(chunk * CHUNK + i * BLOCK)
        hot = ((tp_row[...] == spot).astype(F32) - (tn_row[...] == spot).astype(F32)).astype(BF16)
        return sum(jnp.dot(hot, v, preferred_element_type=F32) for v in values_b)

    def grad_user_term(i):
        hot = (tu_row[...] == spots(i * BLOCK)).astype(F32).astype(BF16)
        return sum(jnp.dot(hot, v, preferred_element_type=F32) for v in upart_split)

    def grad_user_update(value):
        user_base[...] = value
        return (ru[own_u, :] * value).astype(BF16)

    def grad_item_update(value):
        item_base[...] = value
        feeds[3, own_slot, :] = (ri[...] * value).astype(BF16)
        gather_start(3)

    exchange(
        2, grad_item_term, lambda: make_users(grad_user_term), grad_user_update,
        grad_item_update, False,
    )

    def backward(r, carry):
        def user_update(value):
            state = user_base[...] + ru[own_u, :] * value
            return jnp.where(r == 3, ru[own_u, :] * state, state / 3.0).astype(BF16)

        def item_update(value):
            state = item_base[...] + ri[...] * value
            out_item[...] = state / 3.0

            @pl.when(r == 3)
            def _():
                feeds[r + 1, own_slot, :] = (ri[...] * state).astype(BF16)
                gather_start(r + 1)

        exchange(
            r, item_term(r), lambda: make_users(user_term(r)), user_update, item_update, True
        )
        return carry

    lax.fori_loop(3, 5, backward, 0)
    out_user[...] = users[5].astype(F32)


def main(user_emb, item_emb, ru, ri, triples, r_hbm, rt_hbm):
    rows_u, width = user_emb.shape
    col_rows = rt_hbm.shape[0]
    rounds = 5
    quarter = rows_u // SIDE
    vmem = pl.BlockSpec(memory_space=pltpu.VMEM)
    hbm = pl.BlockSpec(memory_space=pl.ANY)
    dma = pltpu.SemaphoreType.DMA
    scratch = [
        pltpu.VMEM((rows_u, col_rows), BF16),
        pltpu.VMEM((col_rows, rows_u), BF16),
        pltpu.VMEM((rounds, col_rows, width), BF16),
        pltpu.VMEM((rounds + 1, rows_u, width), BF16),
        pltpu.VMEM((rounds, SIDE, CHUNK, width), BF16),
        pltpu.VMEM((SIDE, CHUNK, width), BF16),
        pltpu.VMEM((3, CHUNK, width), BF16),
        pltpu.VMEM((rounds, 2, CHUNK // 2, width), BF16),
        pltpu.VMEM((rounds, 2, CHUNK, width), BF16),
        pltpu.VMEM((3, BLOCK, width), BF16),
        pltpu.VMEM((rounds, 2, BLOCK // 2, width), BF16),
        pltpu.VMEM((rounds, 2, BLOCK, width), BF16),
        pltpu.VMEM((3, quarter, width), BF16),
        pltpu.VMEM((rounds, 2, quarter // 2, width), BF16),
        pltpu.VMEM((rounds, 2, quarter, width), BF16),
        pltpu.VMEM((CHUNK, width), F32),
        pltpu.VMEM((rows_u, width), F32),
        pltpu.VMEM((quarter, width), F32),
        pltpu.VMEM((BLOCK, width), F32),
        pltpu.VMEM((quarter, width), F32),
        pltpu.VMEM((BLOCK, width), F32),
        pltpu.VMEM((2, 2 * BLOCK, width), F32),
        dma((2,)),
        dma((rounds, 20)),
        dma((rounds,)),
        dma((rounds, 12)),
        dma((rounds, 3)),
        dma((rounds, 8)),
        dma((rounds, 2)),
    ]
    return pl.pallas_call(
        main_kernel,
        out_shape=(
            jax.ShapeDtypeStruct((rows_u, width), F32),
            jax.ShapeDtypeStruct((BLOCK, width), F32),
        ),
        in_specs=[vmem] * 10 + [hbm] * 2,
        out_specs=(vmem, vmem),
        scratch_shapes=scratch,
        compiler_params=pltpu.CompilerParams(
            collective_id=0, has_side_effects=True, vmem_limit_bytes=60 * 2**20
        ),
        name="propagate",
    )(user_emb, item_emb, ru, ri, *triples, r_hbm, rt_hbm)


def place(block):
    core = block % 2
    x = (block // 2) % SIDE
    y = block // (2 * SIDE)
    return core * SIDE * SIDE + jnp.where(core == 0, y * SIDE + x, x * SIDE + y)


def per_device(
    user_emb, item_emb, user_degree, item_degree, tiles, tile_user, tile_item, tile_count,
    triple_user, triple_pos, triple_neg,
):
    rows_u, width = user_emb.shape[1:]
    col_rows = item_emb.shape[2] * lax.axis_size("user")
    r_mat, rt_mat = build(
        tile_count[0], tile_user[0, 0], place(tile_item[0, 0]), tiles[0, 0], rows_u, col_rows
    )
    ru = jnp.broadcast_to(lax.rsqrt(user_degree[0].astype(F32))[:, None], (rows_u, width))
    ri = jnp.broadcast_to(
        lax.rsqrt(item_degree[0, 0].astype(F32))[:, None], (item_emb.shape[2], width)
    )

    def moved(index):
        return place(index // BLOCK) * BLOCK + index % BLOCK

    picks = (triple_user[0, 0], moved(triple_pos[0, 0]), moved(triple_neg[0, 0]))
    columns = tuple(jnp.broadcast_to(v[:, None], (v.shape[0], BLOCK)) for v in picks)
    lines = tuple(v[None, :] for v in picks)
    grad_user, grad_item = main(
        user_emb[0], item_emb[0, 0], ru, ri, columns + lines, r_mat, rt_mat
    )
    return grad_user[None], grad_item[None, None]


def solution(mesh):
    return jax.shard_map(
        per_device,
        mesh=mesh,
        in_specs=(
            P("user", None, None),
            P("user", "item", None, None),
            P("user", None),
            P("user", "item", None),
            P("user", "item", None, None, None),
            P("user", "item", None),
            P("user", "item", None),
            P("user", "item"),
            P("user", "item", None),
            P("user", "item", None),
            P("user", "item", None),
        ),
        out_specs=(P("user", None, None), P("user", "item", None, None)),
        check_vma=False,
    )
```

```python
import jax
import jax.numpy as jnp
from jax import lax
from jax.experimental import pallas as pl
from jax.experimental.pallas import tpu as pltpu
from jax.sharding import PartitionSpec as P

F32 = jnp.float32
BF16 = jnp.bfloat16
MESH = pl.DeviceIdType.MESH
SIDE = 4
BLOCK = 128
CHUNK = SIDE * BLOCK
HALF = SIDE * CHUNK
ROUNDS = 5
GROUPS = 8


def place(block):
    core = block & 1
    x = (block >> 1) & (SIDE - 1)
    y = block >> 3
    return core * SIDE * SIDE + (y + core * (x - y)) * SIDE + x + core * (y - x)


def build_kernel(count_ref, rows_ref, cols_ref, tiles_hbm, r_ref, tiles, sems):
    slots = tiles.shape[0]
    size = slots // GROUPS
    copies = [
        pltpu.make_async_copy(
            tiles_hbm.at[pl.ds(g * size, size)], tiles.at[pl.ds(g * size, size)], sems.at[g]
        )
        for g in range(GROUPS)
    ]
    for item in copies:
        item.start()
    step = 64

    def clear(i, carry):
        at = pl.ds(pl.multiple_of(i * step, step), step)
        for half in range(2):
            r_ref[half, at, :] = jnp.zeros((step, r_ref.shape[2]), BF16)
        return carry

    lax.fori_loop(0, r_ref.shape[1] // step, clear, 0)

    def add(slot, carry):
        spot = place(cols_ref[slot])
        half = spot // (SIDE * SIDE)
        users = pl.ds(pl.multiple_of(rows_ref[slot] * BLOCK, BLOCK), BLOCK)
        items = pl.ds(pl.multiple_of((spot % (SIDE * SIDE)) * BLOCK, BLOCK), BLOCK)
        tile = tiles[slot].astype(F32)
        r_ref[half, users, items] = (r_ref[half, users, items].astype(F32) + tile).astype(BF16)
        return carry

    count = count_ref[0]
    for g in range(GROUPS):
        copies[g].wait()
        lax.fori_loop(g * size, jnp.clip(count, g * size, (g + 1) * size), add, 0)


def build(count, rows, cols, tiles, users):
    smem = pl.BlockSpec(memory_space=pltpu.SMEM)
    return pl.pallas_call(
        build_kernel,
        out_shape=jax.ShapeDtypeStruct((2, users, HALF), BF16),
        in_specs=[smem, smem, smem, pl.BlockSpec(memory_space=pl.ANY)],
        out_specs=pl.BlockSpec(memory_space=pltpu.VMEM),
        scratch_shapes=[pltpu.VMEM(tiles.shape, jnp.int32), pltpu.SemaphoreType.DMA((GROUPS,))],
        compiler_params=pltpu.CompilerParams(vmem_limit_bytes=16 * 2**20),
        name="build",
    )(count, rows, cols, tiles)


def over_rows(left, right):
    return lax.dot_general(left, right, (((0,), (0,)), ((), ())), preferred_element_type=F32)


def main_kernel(
    user_emb, item_emb, user_degree, item_degree, triple_user, triple_pos, triple_neg, r_mat,
    out_user, out_item,
    feeds, users, sib_in, sib_out, q_out, q_in, p_out, p_in, z_out, z_in,
    part, upart, user_total, item_total, user_base, item_base, pick_u, pick_i, split, ru, ri,
    ag_recv, ag_send, rs_recv, rs_send, z_recv, z_send,
):
    a = lax.axis_index("user")
    z = lax.axis_index("item")
    core = a % 2
    x = (a // 2) % SIDE
    y = a // (2 * SIDE)
    p = x + core * (y - x)
    q = y + core * (x - y)
    rows_u = user_emb.shape[0]
    quarter = rows_u // SIDE
    trips = triple_user.shape[1]

    def at_pq(pp, qq):
        yy = qq + core * (pp - qq)
        xx = pp + core * (qq - pp)
        return {"user": (yy * SIDE + xx) * 2 + core}

    def turn(i, by):
        return (i + by) % SIDE

    to_p = {by: at_pq(turn(p, by), q) for by in (1, 2, 3)}
    to_q = {by: at_pq(p, turn(q, by)) for by in (1, 2, 3)}
    to_z = {by: {"item": turn(z, by)} for by in (1, 2, 3)}
    to_s = {"user": a + 1 - 2 * core}

    def rows(start, count):
        return pl.ds(pl.multiple_of(start, BLOCK), count)

    def copy(src, dst, send, recv, device):
        return pltpu.make_async_remote_copy(
            src_ref=src, dst_ref=dst, send_sem=send, recv_sem=recv,
            device_id=device, device_id_type=MESH,
        )

    barrier = pltpu.get_barrier_semaphore()
    partners = [*to_p.values(), *to_q.values(), *to_z.values(), to_s]
    for device in partners:
        pl.semaphore_signal(barrier, inc=1, device_id=device, device_id_type=MESH)

    def slot(qq, pp):
        return ((core * SIDE + qq) * SIDE + pp) * BLOCK

    def gather_copy(r, start, count, device, recv):
        ref = feeds.at[r, rows(start, count)]
        return copy(ref, ref, ag_send.at[r], ag_recv.at[r, recv], device)

    def to_sibling(r, qq, pp):
        gather_copy(r, slot(qq, pp), BLOCK, to_s, 15 + qq).start()

    def spread_block(r, rel):
        pp = turn(p, rel)
        for by in (2, 1, 3):
            gather_copy(r, slot(q, pp), BLOCK, to_q[by], 3 + (by - 1) * SIDE + rel).start()
        to_sibling(r, q, pp)

    def gather_start(r):
        for by in (2, 1, 3):
            gather_copy(r, slot(q, p), BLOCK, to_p[by], by - 1).start()
        spread_block(r, 0)

    def gather_p(r):
        for by in (1, 3, 2):
            back = turn(p, SIDE - by)
            gather_copy(r, slot(q, back), BLOCK, to_p[by], by - 1).wait_recv()
            spread_block(r, SIDE - by)

    def gather_q(r):
        for rel in (0, 3, 1, 2):
            pp = turn(p, rel)
            for by in (1, 3, 2):
                qq = turn(q, SIDE - by)
                gather_copy(
                    r, slot(qq, pp), BLOCK, to_q[by], 3 + (by - 1) * SIDE + rel
                ).wait_recv()
                to_sibling(r, qq, pp)

    def gather_end(r):
        for other in range(SIDE):
            start = ((1 - core) * SIDE + other) * CHUNK
            gather_copy(r, start, CHUNK, to_s, 15 + other).wait_recv()

    def gather_sent(r):
        gather_copy(r, 0, 31 * BLOCK, to_s, 0).wait_send()

    def feed_half(r, half):
        return feeds[r, rows(half * HALF, HALF), :]

    def sibling_part(r, term, rel):
        theirs = turn(p, rel)
        sib_out[theirs] = term(1 - core, theirs).astype(BF16)
        sibling_copy(r, theirs).start()

    def sibling_copy(r, chunk):
        return copy(
            sib_out.at[chunk], sib_in.at[r, chunk], rs_send.at[r, 0], rs_recv.at[r, chunk], to_s
        )

    def q_copy(r, by, rel):
        at = rows(turn(p, rel) * BLOCK, BLOCK)
        return copy(
            q_out.at[by - 1, at], q_in.at[r, by - 1, at], rs_send.at[r, 1],
            rs_recv.at[r, 4 + (by - 1) * SIDE + rel], to_q[by],
        )

    def p_copy(r, by):
        return copy(
            p_out.at[by - 1], p_in.at[r, by - 1], rs_send.at[r, 2],
            rs_recv.at[r, 15 + by], to_p[by],
        )

    def own_part(r, term, by):
        chunk = turn(q, by)
        part[...] = term(core, chunk)
        sibling_copy(r, chunk).wait_recv()
        value = part[...] + sib_in[r, chunk].astype(F32)
        if by == 0:
            part[...] = value
        else:
            q_out[by - 1] = value.astype(BF16)

    def q_send(r, bys, rels):
        for rel in rels:
            for by in bys:
                q_copy(r, by, rel).start()

    def sum_make(r, term, hook=None):
        if hook is None:
            for by in (2, 1, 3):
                sibling_part(r, term, by)
                own_part(r, term, by)
                q_send(r, (by,), (2, 1))
            q_send(r, (2, 1, 3), (3, 0))
            sibling_part(r, term, 0)
        else:
            for by in (2, 1, 3, 0):
                sibling_part(r, term, by)
            for by in (2, 1, 3):
                own_part(r, term, by)
            hook()
            q_send(r, (2, 1, 3), (2, 1, 3, 0))
        own_part(r, term, 0)

    def sum_q(r, rel):
        at = rows(turn(p, rel) * BLOCK, BLOCK)
        value = part[at, :]
        for by in (1, 3, 2):
            q_copy(r, by, rel).wait_recv()
            value = value + q_in[r, by - 1, at, :].astype(F32)
        return value

    def sum_p(r):
        for by in (2, 1, 3):
            p_out[by - 1] = sum_q(r, by).astype(BF16)
            p_copy(r, by).start()

    def sum_end(r):
        value = sum_q(r, 0)
        for by in (1, 3, 2):
            p_copy(r, by).wait_recv()
            value = value + p_in[r, by - 1].astype(F32)
        return value

    def sums_sent(r):
        copy(sib_out, sib_in.at[r], rs_send.at[r, 0], rs_recv.at[r, 0], to_s).wait_send()
        copy(q_out, q_in.at[r], rs_send.at[r, 1], rs_recv.at[r, 4], to_q[1]).wait_send()
        copy(p_out, p_in.at[r], rs_send.at[r, 2], rs_recv.at[r, 16], to_p[1]).wait_send()

    def z_copy(r, by):
        return copy(
            z_out.at[by - 1], z_in.at[r, by - 1], z_send.at[r, 0], z_recv.at[r, by - 1], to_z[by]
        )

    def u_copy(r, owner, by):
        ref = users.at[r + 1, rows(owner * quarter, quarter)]
        return copy(ref, ref, z_send.at[r, 1], z_recv.at[r, 2 + by], to_z[by])

    def users_make(r, term):
        for by in (2, 1, 3, 0):
            value = term(turn(z, by))
            if by == 0:
                upart[rows(z * quarter, quarter), :] = value
            else:
                z_out[by - 1] = value.astype(BF16)
                z_copy(r, by).start()

    def user_end(r):
        value = upart[rows(z * quarter, quarter), :]
        for by in (1, 3, 2):
            z_copy(r, by).wait_recv()
            value = value + z_in[r, by - 1].astype(F32)
        return value

    def user_spread(r, value):
        users[r + 1, rows(z * quarter, quarter), :] = value
        for by in (2, 1, 3):
            u_copy(r, z, by).start()

    def user_ready(r):
        for by in (1, 3, 2):
            u_copy(r, turn(z, SIDE - by), by).wait_recv()

    def users_sent(r):
        copy(z_out, z_in.at[r], z_send.at[r, 0], z_recv.at[r, 0], to_z[1]).wait_send()
        ref = users.at[r + 1, pl.ds(0, 3 * quarter)]
        copy(ref, ref, z_send.at[r, 1], z_recv.at[r, 3], to_z[1]).wait_send()

    def item_term(r):
        def term(half, chunk):
            return over_rows(r_mat[half, :, rows(chunk * CHUNK, CHUNK)], users[r])

        return term

    def users_first(r):
        def step(i, carry):
            at = rows(i * CHUNK, CHUNK)
            upart[at, :] = jnp.dot(
                r_mat[core, at, :], feed_half(r, core), preferred_element_type=F32
            )
            return carry

        lax.fori_loop(0, rows_u // CHUNK, step, 0)

    def user_term(r):
        def term(owner):
            at = rows(owner * quarter, quarter)
            return upart[at, :] + jnp.dot(
                r_mat[1 - core, at, :], feed_half(r, 1 - core), preferred_element_type=F32
            )

        return term

    def column(line):
        return jnp.broadcast_to(line, (BLOCK, BLOCK)).T

    def wide(scale):
        return jnp.concatenate([scale, scale], axis=1)

    own_u = rows(z * quarter, quarter)
    own_slot = rows(slot(q, p), BLOCK)

    def ru_own():
        return wide(ru[own_u, :])

    def ri_own():
        return wide(ri[...])

    ri[...] = column(lax.rsqrt(item_degree[...].astype(F32)))
    ei = item_emb[...].astype(F32)
    feeds[0, own_slot, :] = (ri_own() * ei).astype(BF16)
    pl.semaphore_wait(barrier, len(partners))
    gather_start(0)
    item_total[...] = ei
    for i in range(rows_u // BLOCK):
        at = slice(i * BLOCK, (i + 1) * BLOCK)
        scale = column(lax.rsqrt(user_degree[:, at].astype(F32)))
        ru[at, :] = scale
        users[0, at, :] = (wide(scale) * user_emb[at, :].astype(F32)).astype(BF16)
    user_total[...] = user_emb[own_u, :].astype(F32)

    def make_picks():
        def spot(ref):
            value = ref[...]
            return place(value >> 7) * BLOCK + (value & (BLOCK - 1))

        def columns(line):
            line = line.astype(F32)
            return jnp.concatenate(
                [column(line[:, i : i + BLOCK]) for i in range(0, trips, BLOCK)], axis=0
            )

        lane = lax.broadcasted_iota(jnp.int32, (trips, BLOCK), 1).astype(F32)
        chosen = columns(triple_user[...])
        for i in range(rows_u // BLOCK):
            hot = (chosen - i * BLOCK == lane).astype(F32)
            pick_u[:, i * BLOCK : (i + 1) * BLOCK] = hot.astype(BF16)
        pos = columns(spot(triple_pos))
        neg = columns(spot(triple_neg))
        for half in range(2):
            for i in range(HALF // BLOCK):
                at = half * HALF + i * BLOCK
                hot = (pos - at == lane).astype(F32) - (neg - at == lane).astype(F32)
                pick_i[half, :, i * BLOCK : (i + 1) * BLOCK] = hot.astype(BF16)

    def two_rounds(r, user_update, item_update, between):
        sum_make(r, item_term(r), lambda: gather_p(r))
        gather_q(r)
        users_first(r)
        gather_end(r)
        users_make(r, user_term(r))
        sum_p(r)
        item_update(r, sum_end(r))
        gather_start(r + 1)
        gather_p(r + 1)
        user_spread(r, user_update(r, user_end(r)))
        users_sent(r)
        sums_sent(r)
        between()
        gather_q(r + 1)
        users_first(r + 1)
        gather_end(r + 1)
        users_make(r + 1, user_term(r + 1))
        user_ready(r)
        sum_make(r + 1, item_term(r + 1))
        user_spread(r + 1, user_update(r + 1, user_end(r + 1)))
        sum_p(r + 1)
        item_update(r + 1, sum_end(r + 1))

    def forward_user(r, value):
        state = (ru_own() * value).astype(BF16).astype(F32)
        user_total[...] += state
        feed = ru_own() * state if r == 0 else user_total[...] / 3.0
        return feed.astype(BF16)

    def forward_item(r, value):
        state = (ri_own() * value).astype(BF16).astype(F32)
        item_total[...] += state
        feed = ri_own() * state if r == 0 else item_total[...] / 3.0
        feeds[r + 1, own_slot, :] = feed.astype(BF16)

    two_rounds(0, forward_user, forward_item, make_picks)

    gather_start(2)
    users_sent(1)
    sums_sent(1)
    gather_p(2)
    user_ready(1)
    user_rows = jnp.dot(pick_u[...], users[2], preferred_element_type=F32)
    upart[:trips, :] = user_rows
    gather_q(2)
    upart[trips : 2 * trips, :] = jnp.dot(
        pick_i[core], feed_half(2, core), preferred_element_type=F32
    )
    gather_end(2)
    diff = upart[trips : 2 * trips, :] + jnp.dot(
        pick_i[1 - core], feed_half(2, 1 - core), preferred_element_type=F32
    )
    user_rows = upart[:trips, :]
    score = jnp.sum(user_rows * diff, axis=1, keepdims=True)
    weight = -jax.nn.sigmoid(-score)
    for i, value in enumerate((weight * diff, weight * user_rows)):
        high = value.astype(BF16)
        split[i, :, :256] = high
        split[i, :, 256:] = (value - high.astype(F32)).astype(BF16)

    def both(product):
        return product[:, :256] + product[:, 256:]

    def grad_user_term(owner):
        return both(over_rows(pick_u[:, rows(owner * quarter, quarter)], split[0]))

    def grad_item_term(half, chunk):
        return both(over_rows(pick_i[half, :, rows(chunk * CHUNK, CHUNK)], split[1]))

    users_make(2, grad_user_term)
    sum_make(2, grad_item_term)
    value = user_end(2)
    user_base[...] = value
    user_spread(2, (ru_own() * value).astype(BF16))
    sum_p(2)
    value = sum_end(2)
    item_base[...] = value
    feeds[3, own_slot, :] = (ri_own() * value).astype(BF16)
    gather_start(3)
    users_sent(2)
    sums_sent(2)
    user_ready(2)

    def backward_user(r, value):
        state = user_base[...] + ru_own() * value
        return (ru_own() * state if r == 3 else state / 3.0).astype(BF16)

    def backward_item(r, value):
        state = item_base[...] + ri_own() * value
        if r == 3:
            feeds[r + 1, own_slot, :] = (ri_own() * state).astype(BF16)
        else:
            out_item[...] = state / 3.0

    two_rounds(3, backward_user, backward_item, lambda: None)
    user_ready(4)
    out_user[...] = users[5]
    users_sent(4)
    sums_sent(4)
    for r in range(ROUNDS):
        gather_sent(r)


def main(user_emb, item_emb, user_degree, item_degree, triples, r_mat):
    rows_u, width = user_emb.shape
    col_rows = 2 * HALF
    quarter = rows_u // SIDE
    trips = triples[0].shape[1]
    vmem = pl.BlockSpec(memory_space=pltpu.VMEM)
    dma = pltpu.SemaphoreType.DMA
    scratch = [
        pltpu.VMEM((ROUNDS, col_rows, width), BF16),
        pltpu.VMEM((ROUNDS + 1, rows_u, width), BF16),
        pltpu.VMEM((ROUNDS, SIDE, CHUNK, width), BF16),
        pltpu.VMEM((SIDE, CHUNK, width), BF16),
        pltpu.VMEM((3, CHUNK, width), BF16),
        pltpu.VMEM((ROUNDS, 3, CHUNK, width), BF16),
        pltpu.VMEM((3, BLOCK, width), BF16),
        pltpu.VMEM((ROUNDS, 3, BLOCK, width), BF16),
        pltpu.VMEM((3, quarter, width), BF16),
        pltpu.VMEM((ROUNDS, 3, quarter, width), BF16),
        pltpu.VMEM((CHUNK, width), F32),
        pltpu.VMEM((rows_u, width), F32),
        pltpu.VMEM((quarter, width), F32),
        pltpu.VMEM((BLOCK, width), F32),
        pltpu.VMEM((quarter, width), F32),
        pltpu.VMEM((BLOCK, width), F32),
        pltpu.VMEM((trips, rows_u), BF16),
        pltpu.VMEM((2, trips, HALF), BF16),
        pltpu.VMEM((2, trips, 2 * width), BF16),
        pltpu.VMEM((rows_u, BLOCK), F32),
        pltpu.VMEM((BLOCK, BLOCK), F32),
        dma((ROUNDS, 19)),
        dma((ROUNDS,)),
        dma((ROUNDS, 19)),
        dma((ROUNDS, 3)),
        dma((ROUNDS, 6)),
        dma((ROUNDS, 2)),
    ]
    return pl.pallas_call(
        main_kernel,
        out_shape=(
            jax.ShapeDtypeStruct((rows_u, width), BF16),
            jax.ShapeDtypeStruct((BLOCK, width), F32),
        ),
        in_specs=[vmem] * 8,
        out_specs=(vmem, vmem),
        scratch_shapes=scratch,
        compiler_params=pltpu.CompilerParams(
            collective_id=0, has_side_effects=True, vmem_limit_bytes=44 * 2**20
        ),
        name="propagate",
    )(user_emb, item_emb, user_degree, item_degree, *triples, r_mat)


def finish_kernel(user, item, out_user, out_item):
    out_user[...] = user[...].astype(F32)
    out_item[...] = item[...]


def finish(user, item):
    vmem = pl.BlockSpec(memory_space=pltpu.VMEM)
    return pl.pallas_call(
        finish_kernel,
        out_shape=(
            jax.ShapeDtypeStruct(user.shape, F32),
            jax.ShapeDtypeStruct(item.shape, F32),
        ),
        in_specs=[vmem, vmem],
        out_specs=(vmem, vmem),
        name="finish",
    )(user, item)


def per_device(
    user_emb, item_emb, user_degree, item_degree, tiles, tile_user, tile_item, tile_count,
    triple_user, triple_pos, triple_neg,
):
    r_mat = build(tile_count[0], tile_user[0, 0], tile_item[0, 0], tiles[0, 0], user_emb.shape[1])
    grad_user, grad_item = finish(*main(
        user_emb[0], item_emb[0, 0], user_degree, item_degree[0],
        (triple_user[0], triple_pos[0], triple_neg[0]), r_mat,
    ))
    return grad_user[None], grad_item[None, None]


def solution(mesh):
    return jax.shard_map(
        per_device,
        mesh=mesh,
        in_specs=(
            P("user", None, None),
            P("user", "item", None, None),
            P("user", None),
            P("user", "item", None),
            P("user", "item", None, None, None),
            P("user", "item", None),
            P("user", "item", None),
            P("user", "item"),
            P("user", "item", None),
            P("user", "item", None),
            P("user", "item", None),
        ),
        out_specs=(P("user", None, None), P("user", "item", None, None)),
        check_vma=False,
    )
```

```python
import jax
import jax.numpy as jnp
from jax import lax
from jax.experimental import pallas as pl
from jax.experimental.pallas import tpu as pltpu
from jax.sharding import PartitionSpec as P

F32 = jnp.float32
BF16 = jnp.bfloat16
MESH = pl.DeviceIdType.MESH
SIDE = 4
BLOCK = 128
CHUNK = SIDE * BLOCK
HALF = SIDE * CHUNK
ROUNDS = 5
GROUPS = 8


def place(block):
    core = block & 1
    x = (block >> 1) & (SIDE - 1)
    y = block >> 3
    return core * SIDE * SIDE + (y + core * (x - y)) * SIDE + x + core * (y - x)


def build_kernel(
    count_hbm, rows_hbm, cols_hbm, tiles_hbm, r_ref, count_ref, rows_ref, cols_ref, tiles, sems
):
    slots = tiles.shape[0]
    scalars = [
        pltpu.make_async_copy(src, dst, sems.at[GROUPS + i])
        for i, (src, dst) in enumerate(
            ((count_hbm, count_ref), (rows_hbm, rows_ref), (cols_hbm, cols_ref))
        )
    ]
    for item in scalars:
        item.start()
    size = slots // GROUPS
    copies = [
        pltpu.make_async_copy(
            tiles_hbm.at[pl.ds(g * size, size)], tiles.at[pl.ds(g * size, size)], sems.at[g]
        )
        for g in range(GROUPS)
    ]
    for item in copies:
        item.start()
    step = 64

    def clear(i, carry):
        at = pl.ds(pl.multiple_of(i * step, step), step)
        for half in range(2):
            r_ref[half, at, :] = jnp.zeros((step, r_ref.shape[2]), BF16)
        return carry

    lax.fori_loop(0, r_ref.shape[1] // step, clear, 0)

    def add(slot, carry):
        spot = place(cols_ref[0, slot])
        half = spot // (SIDE * SIDE)
        users = pl.ds(pl.multiple_of(rows_ref[0, slot] * BLOCK, BLOCK), BLOCK)
        items = pl.ds(pl.multiple_of((spot % (SIDE * SIDE)) * BLOCK, BLOCK), BLOCK)
        tile = tiles[slot].astype(F32)
        r_ref[half, users, items] = (r_ref[half, users, items].astype(F32) + tile).astype(BF16)
        return carry

    for item in scalars:
        item.wait()
    count = count_ref[0, 0]
    for g in range(GROUPS):
        copies[g].wait()
        lax.fori_loop(g * size, jnp.clip(count, g * size, (g + 1) * size), add, 0)


def build(count, rows, cols, tiles, users):
    hbm = pl.BlockSpec(memory_space=pl.ANY)
    return pl.pallas_call(
        build_kernel,
        out_shape=jax.ShapeDtypeStruct((2, users, HALF), BF16),
        in_specs=[hbm] * 4,
        out_specs=pl.BlockSpec(memory_space=pltpu.VMEM),
        scratch_shapes=[
            pltpu.SMEM(count.shape, jnp.int32),
            pltpu.SMEM(rows.shape, jnp.int32),
            pltpu.SMEM(cols.shape, jnp.int32),
            pltpu.VMEM(tiles.shape, jnp.int32),
            pltpu.SemaphoreType.DMA((GROUPS + 3,)),
        ],
        compiler_params=pltpu.CompilerParams(vmem_limit_bytes=16 * 2**20),
        name="build",
    )(count, rows, cols, tiles)


def over_rows(left, right):
    return lax.dot_general(left, right, (((0,), (0,)), ((), ())), preferred_element_type=F32)


def main_kernel(
    user_emb_hbm, item_emb_hbm, user_degree_hbm, item_degree_hbm, triple_user_hbm,
    triple_pos_hbm, triple_neg_hbm, r_mat,
    out_user, out_item,
    user_emb, item_emb, user_degree, item_degree, triple_user, triple_pos, triple_neg,
    feeds, users, sib_in, sib_out, q_out, q_in, p_out, p_in, z_out, z_in,
    part, upart, user_total, item_total, user_base, item_base, pick_u, pick_i, split, ru, ri,
    load_sem, ag_recv, ag_send, rs_recv, rs_send, z_recv, z_send,
):
    a = lax.axis_index("user")
    z = lax.axis_index("item")
    core = a % 2
    x = (a // 2) % SIDE
    y = a // (2 * SIDE)
    p = x + core * (y - x)
    q = y + core * (x - y)
    rows_u = user_emb.shape[0]
    quarter = rows_u // SIDE
    trips = triple_user.shape[1]
    half_q = quarter // 2

    def at_pq(pp, qq):
        yy = qq + core * (pp - qq)
        xx = pp + core * (qq - pp)
        return {"user": (yy * SIDE + xx) * 2 + core}

    def turn(i, by):
        return (i + by) % SIDE

    to_p = {by: at_pq(turn(p, by), q) for by in (1, 2, 3)}
    to_q = {by: at_pq(p, turn(q, by)) for by in (1, 2, 3)}
    to_z = {by: {"item": turn(z, by)} for by in (1, 2, 3)}
    to_s = {"user": a + 1 - 2 * core}

    def rows(start, count):
        return pl.ds(pl.multiple_of(start, BLOCK), count)

    def copy(src, dst, send, recv, device):
        return pltpu.make_async_remote_copy(
            src_ref=src, dst_ref=dst, send_sem=send, recv_sem=recv,
            device_id=device, device_id_type=MESH,
        )

    loads = [
        pltpu.make_async_copy(src, dst, load_sem.at[i])
        for i, (src, dst) in enumerate((
            (item_degree_hbm, item_degree), (item_emb_hbm, item_emb),
            (user_degree_hbm, user_degree), (user_emb_hbm, user_emb),
            (triple_user_hbm, triple_user), (triple_pos_hbm, triple_pos),
            (triple_neg_hbm, triple_neg),
        ))
    ]
    for load in loads:
        load.start()
    barrier = pltpu.get_barrier_semaphore()
    partners = [*to_p.values(), *to_q.values(), *to_z.values(), to_s]
    for device in partners:
        pl.semaphore_signal(barrier, inc=1, device_id=device, device_id_type=MESH)

    def slot(qq, pp):
        return ((core * SIDE + qq) * SIDE + pp) * BLOCK

    def gather_copy(r, start, count, device, recv):
        ref = feeds.at[r, rows(start, count)]
        return copy(ref, ref, ag_send.at[r], ag_recv.at[r, recv], device)

    def to_sibling(r, qq, pp):
        gather_copy(r, slot(qq, pp), BLOCK, to_s, 15 + qq).start()

    def spread_block(r, rel):
        pp = turn(p, rel)
        for by in (2, 1, 3):
            gather_copy(r, slot(q, pp), BLOCK, to_q[by], 3 + (by - 1) * SIDE + rel).start()
        to_sibling(r, q, pp)

    def gather_start(r):
        for by in (2, 1, 3):
            gather_copy(r, slot(q, p), BLOCK, to_p[by], by - 1).start()
        spread_block(r, 0)

    def gather_p(r):
        for by in (1, 3, 2):
            back = turn(p, SIDE - by)
            gather_copy(r, slot(q, back), BLOCK, to_p[by], by - 1).wait_recv()
            spread_block(r, SIDE - by)

    def gather_q(r, hook=None):
        for rel in (0, 3, 1, 2):
            if rel == 1 and hook is not None:
                hook()
            pp = turn(p, rel)
            for by in (1, 3, 2):
                qq = turn(q, SIDE - by)
                gather_copy(
                    r, slot(qq, pp), BLOCK, to_q[by], 3 + (by - 1) * SIDE + rel
                ).wait_recv()
                to_sibling(r, qq, pp)

    def gather_end(r):
        for other in range(SIDE):
            start = ((1 - core) * SIDE + other) * CHUNK
            gather_copy(r, start, CHUNK, to_s, 15 + other).wait_recv()

    def gather_sent(r):
        gather_copy(r, 0, 31 * BLOCK, to_s, 0).wait_send()

    def feed_half(r, half):
        return feeds[r, rows(half * HALF, HALF), :]

    def sibling_part(r, term, rel):
        theirs = turn(p, rel)
        sib_out[theirs] = term(1 - core, theirs).astype(BF16)
        sibling_copy(r, theirs).start()

    def sibling_copy(r, chunk):
        return copy(
            sib_out.at[chunk], sib_in.at[r, chunk], rs_send.at[r, 0], rs_recv.at[r, chunk], to_s
        )

    def q_copy(r, by, rel):
        at = rows(turn(p, rel) * BLOCK, BLOCK)
        return copy(
            q_out.at[by - 1, at], q_in.at[r, by - 1, at], rs_send.at[r, 1],
            rs_recv.at[r, 4 + (by - 1) * SIDE + rel], to_q[by],
        )

    def p_copy(r, by):
        return copy(
            p_out.at[by - 1], p_in.at[r, by - 1], rs_send.at[r, 2],
            rs_recv.at[r, 15 + by], to_p[by],
        )

    def own_part(r, term, by):
        chunk = turn(q, by)
        part[...] = term(core, chunk)
        sibling_copy(r, chunk).wait_recv()
        value = part[...] + sib_in[r, chunk].astype(F32)
        if by == 0:
            part[...] = value
        else:
            q_out[by - 1] = value.astype(BF16)

    def q_send(r, bys, rels):
        for rel in rels:
            for by in bys:
                q_copy(r, by, rel).start()

    def sum_make(r, term):
        sibling_part(r, term, 2)
        for by, later in ((2, 1), (1, 3), (3, 0)):
            sibling_part(r, term, later)
            own_part(r, term, by)
            q_send(r, (by,), (2, 1))
        q_send(r, (2, 1, 3), (3, 0))
        own_part(r, term, 0)

    def sum_q(r, rel):
        at = rows(turn(p, rel) * BLOCK, BLOCK)
        value = part[at, :]
        for by in (1, 3, 2):
            q_copy(r, by, rel).wait_recv()
            value = value + q_in[r, by - 1, at, :].astype(F32)
        return value

    def sum_p(r):
        for by in (2, 1, 3):
            p_out[by - 1] = sum_q(r, by).astype(BF16)
            p_copy(r, by).start()

    def sum_end(r):
        value = sum_q(r, 0)
        for by in (1, 3, 2):
            p_copy(r, by).wait_recv()
            value = value + p_in[r, by - 1].astype(F32)
        return value

    def sums_sent(r):
        copy(sib_out, sib_in.at[r], rs_send.at[r, 0], rs_recv.at[r, 0], to_s).wait_send()
        copy(q_out, q_in.at[r], rs_send.at[r, 1], rs_recv.at[r, 4], to_q[1]).wait_send()
        copy(p_out, p_in.at[r], rs_send.at[r, 2], rs_recv.at[r, 16], to_p[1]).wait_send()

    def z_copy(r, by, sub):
        at = rows(sub * half_q, half_q)
        return copy(
            z_out.at[by - 1, at], z_in.at[r, by - 1, at], z_send.at[r, 0],
            z_recv.at[r, (by - 1) * 2 + sub], to_z[by],
        )

    def u_copy(r, owner, by, sub):
        ref = users.at[r + 1, rows(owner * quarter + sub * half_q, half_q)]
        return copy(ref, ref, z_send.at[r, 1], z_recv.at[r, 4 + by * 2 + sub], to_z[by])

    def users_make(r, term):
        for by in (2, 1, 3):
            z_out[by - 1] = term(turn(z, by)).astype(BF16)
            z_copy(r, by, 0).start()
        for by in (2, 1, 3):
            z_copy(r, by, 1).start()
        upart[rows(z * quarter, quarter), :] = term(z)

    def user_turn(r, sub, update):
        at = rows(z * quarter + sub * half_q, half_q)
        own = slice(sub * half_q, (sub + 1) * half_q)
        value = upart[at, :]
        for by in (1, 3, 2):
            z_copy(r, by, sub).wait_recv()
            value = value + z_in[r, by - 1, own, :].astype(F32)
        users[r + 1, at, :] = update(r, own, wide(ru[at, :]), value).astype(BF16)
        for by in (2, 1, 3):
            u_copy(r, z, by, sub).start()

    def user_ready(r):
        for sub in range(2):
            for by in (1, 3, 2):
                u_copy(r, turn(z, SIDE - by), by, sub).wait_recv()

    def z_sent(r):
        copy(z_out, z_in.at[r], z_send.at[r, 0], z_recv.at[r, 0], to_z[1]).wait_send()

    def u_sent(r):
        ref = users.at[r + 1, pl.ds(0, 3 * quarter)]
        copy(ref, ref, z_send.at[r, 1], z_recv.at[r, 6], to_z[1]).wait_send()

    def item_term(r):
        def term(half, chunk):
            return over_rows(r_mat[half, :, rows(chunk * CHUNK, CHUNK)], users[r])

        return term

    def users_first(r):
        def step(i, carry):
            at = rows(i * CHUNK, CHUNK)
            upart[at, :] = jnp.dot(
                r_mat[core, at, :], feed_half(r, core), preferred_element_type=F32
            )
            return carry

        lax.fori_loop(0, rows_u // CHUNK, step, 0)

    def user_term(r):
        def term(owner):
            at = rows(owner * quarter, quarter)
            return upart[at, :] + jnp.dot(
                r_mat[1 - core, at, :], feed_half(r, 1 - core), preferred_element_type=F32
            )

        return term

    def column(line):
        return jnp.broadcast_to(line, (BLOCK, BLOCK)).T

    def wide(scale):
        return jnp.concatenate([scale, scale], axis=1)

    own_u = rows(z * quarter, quarter)
    own_slot = rows(slot(q, p), BLOCK)

    def ri_own():
        return wide(ri[...])

    for load in loads[:2]:
        load.wait()
    ri[...] = column(lax.rsqrt(item_degree[...].astype(F32)))
    ei = item_emb[...].astype(F32)
    feeds[0, own_slot, :] = (ri_own() * ei).astype(BF16)
    pl.semaphore_wait(barrier, len(partners))
    gather_start(0)
    item_total[...] = ei
    for load in loads[2:]:
        load.wait()
    for i in range(rows_u // BLOCK):
        at = slice(i * BLOCK, (i + 1) * BLOCK)
        scale = column(lax.rsqrt(user_degree[:, at].astype(F32)))
        ru[at, :] = scale
        users[0, at, :] = (wide(scale) * user_emb[at, :].astype(F32)).astype(BF16)
    user_total[...] = user_emb[own_u, :].astype(F32)

    def make_picks():
        def spot(ref):
            value = ref[...]
            return place(value >> 7) * BLOCK + (value & (BLOCK - 1))

        def columns(line):
            line = line.astype(F32)
            return jnp.concatenate(
                [column(line[:, i : i + BLOCK]) for i in range(0, trips, BLOCK)], axis=0
            )

        lane = lax.broadcasted_iota(jnp.int32, (trips, BLOCK), 1).astype(F32)
        chosen = columns(triple_user[...])
        for i in range(rows_u // BLOCK):
            hot = (chosen - i * BLOCK == lane).astype(F32)
            pick_u[:, i * BLOCK : (i + 1) * BLOCK] = hot.astype(BF16)
        pos = columns(spot(triple_pos))
        neg = columns(spot(triple_neg))
        for half in range(2):
            for i in range(HALF // BLOCK):
                at = half * HALF + i * BLOCK
                hot = (pos - at == lane).astype(F32) - (neg - at == lane).astype(F32)
                pick_i[half, :, i * BLOCK : (i + 1) * BLOCK] = hot.astype(BF16)

    def users_last(r):
        gather_end(r)
        if r > 0:
            z_sent(r - 1)
        users_make(r, user_term(r))

    def forward_user(r, own, scale, value):
        state = (scale * value).astype(BF16).astype(F32)
        user_total[own, :] += state
        return scale * state if r == 0 else user_total[own, :] / 3.0

    def forward_item(r, value):
        state = (ri_own() * value).astype(BF16).astype(F32)
        item_total[...] += state
        feed = ri_own() * state if r == 0 else item_total[...] / 3.0
        feeds[r + 1, own_slot, :] = feed.astype(BF16)
        gather_start(r + 1)

    term = item_term(0)
    for by in (2, 1, 3, 0):
        sibling_part(0, term, by)
    gather_p(0)
    for by in (2, 1, 3, 0):
        own_part(0, term, by)
    gather_q(0, lambda: q_send(0, (2, 1, 3), (2, 1, 3, 0)))
    users_first(0)
    users_last(0)
    sum_p(0)
    forward_item(0, sum_end(0))
    user_turn(0, 0, forward_user)
    user_turn(0, 1, forward_user)
    make_picks()
    gather_p(1)
    sums_sent(0)
    user_ready(0)
    sum_make(1, item_term(1))
    gather_q(1)
    users_first(1)
    sum_p(1)
    users_last(1)
    forward_item(1, sum_end(1))
    user_turn(1, 0, forward_user)
    user_turn(1, 1, forward_user)

    gather_p(2)
    gather_q(2)
    user_ready(1)
    upart[:trips, :] = jnp.dot(pick_u[...], users[2], preferred_element_type=F32)
    upart[trips : 2 * trips, :] = jnp.dot(
        pick_i[core], feed_half(2, core), preferred_element_type=F32
    )
    gather_end(2)
    diff = upart[trips : 2 * trips, :] + jnp.dot(
        pick_i[1 - core], feed_half(2, 1 - core), preferred_element_type=F32
    )
    user_rows = upart[:trips, :]
    score = jnp.sum(user_rows * diff, axis=1, keepdims=True)
    weight = -jax.nn.sigmoid(-score)
    for i, value in enumerate((weight * diff, weight * user_rows)):
        high = value.astype(BF16)
        split[i, :, :256] = high
        split[i, :, 256:] = (value - high.astype(F32)).astype(BF16)

    def both(product):
        return product[:, :256] + product[:, 256:]

    def grad_user_term(owner):
        return both(over_rows(pick_u[:, rows(owner * quarter, quarter)], split[0]))

    def grad_item_term(half, chunk):
        return both(over_rows(pick_i[half, :, rows(chunk * CHUNK, CHUNK)], split[1]))

    def grad_user(r, own, scale, value):
        user_base[own, :] = value
        return scale * value

    z_sent(1)
    users_make(2, grad_user_term)
    sums_sent(1)
    sum_make(2, grad_item_term)
    user_turn(2, 0, grad_user)
    user_turn(2, 1, grad_user)
    sum_p(2)
    value = sum_end(2)
    item_base[...] = value
    feeds[3, own_slot, :] = (ri_own() * value).astype(BF16)
    gather_start(3)

    def backward_user(r, own, scale, value):
        state = user_base[own, :] + scale * value
        return scale * state if r == 3 else state / 3.0

    sums_sent(2)
    user_ready(2)
    sum_make(3, item_term(3))
    gather_p(3)
    gather_q(3, lambda: sum_p(3))
    state = item_base[...] + ri_own() * sum_end(3)
    feeds[4, own_slot, :] = (ri_own() * state).astype(BF16)
    gather_start(4)
    users_first(3)
    users_last(3)
    gather_p(4)
    user_turn(3, 0, backward_user)
    user_turn(3, 1, backward_user)
    gather_q(4)
    users_first(4)
    users_last(4)
    sums_sent(3)
    user_ready(3)
    sum_make(4, item_term(4))
    user_turn(4, 0, backward_user)
    user_turn(4, 1, backward_user)
    sum_p(4)
    out_item[...] = item_base[...] + ri_own() * sum_end(4)
    user_ready(4)
    out_user[...] = users[5]
    sums_sent(4)
    z_sent(4)
    for r in range(ROUNDS):
        u_sent(r)
        gather_sent(r)


def main(user_emb, item_emb, user_degree, item_degree, triples, r_mat):
    rows_u, width = user_emb.shape
    col_rows = 2 * HALF
    quarter = rows_u // SIDE
    trips = triples[0].shape[1]
    vmem = pl.BlockSpec(memory_space=pltpu.VMEM)
    dma = pltpu.SemaphoreType.DMA
    small = (user_emb, item_emb, user_degree, item_degree, *triples)
    scratch = [pltpu.VMEM(v.shape, v.dtype) for v in small] + [
        pltpu.VMEM((ROUNDS, col_rows, width), BF16),
        pltpu.VMEM((ROUNDS + 1, rows_u, width), BF16),
        pltpu.VMEM((ROUNDS, SIDE, CHUNK, width), BF16),
        pltpu.VMEM((SIDE, CHUNK, width), BF16),
        pltpu.VMEM((3, CHUNK, width), BF16),
        pltpu.VMEM((ROUNDS, 3, CHUNK, width), BF16),
        pltpu.VMEM((3, BLOCK, width), BF16),
        pltpu.VMEM((ROUNDS, 3, BLOCK, width), BF16),
        pltpu.VMEM((3, quarter, width), BF16),
        pltpu.VMEM((ROUNDS, 3, quarter, width), BF16),
        pltpu.VMEM((CHUNK, width), F32),
        pltpu.VMEM((rows_u, width), F32),
        pltpu.VMEM((quarter, width), F32),
        pltpu.VMEM((BLOCK, width), F32),
        pltpu.VMEM((quarter, width), F32),
        pltpu.VMEM((BLOCK, width), F32),
        pltpu.VMEM((trips, rows_u), BF16),
        pltpu.VMEM((2, trips, HALF), BF16),
        pltpu.VMEM((2, trips, 2 * width), BF16),
        pltpu.VMEM((rows_u, BLOCK), F32),
        pltpu.VMEM((BLOCK, BLOCK), F32),
        dma((7,)),
        dma((ROUNDS, 19)),
        dma((ROUNDS,)),
        dma((ROUNDS, 19)),
        dma((ROUNDS, 3)),
        dma((ROUNDS, 12)),
        dma((ROUNDS, 2)),
    ]
    return pl.pallas_call(
        main_kernel,
        out_shape=(
            jax.ShapeDtypeStruct((rows_u, width), BF16),
            jax.ShapeDtypeStruct((BLOCK, width), F32),
        ),
        in_specs=[pl.BlockSpec(memory_space=pl.ANY)] * 7 + [vmem],
        out_specs=(vmem, vmem),
        scratch_shapes=scratch,
        compiler_params=pltpu.CompilerParams(
            collective_id=0, has_side_effects=True, vmem_limit_bytes=44 * 2**20
        ),
        name="propagate",
    )(*small, r_mat)


def per_device(
    user_emb, item_emb, user_degree, item_degree, tiles, tile_user, tile_item, tile_count,
    triple_user, triple_pos, triple_neg,
):
    r_mat = build(tile_count, tile_user[0], tile_item[0], tiles[0, 0], user_emb.shape[1])
    grad_user, grad_item = main(
        user_emb[0], item_emb[0, 0], user_degree, item_degree[0],
        (triple_user[0], triple_pos[0], triple_neg[0]), r_mat,
    )
    return grad_user.astype(F32)[None], (grad_item / 3.0)[None, None]


def solution(mesh):
    return jax.shard_map(
        per_device,
        mesh=mesh,
        in_specs=(
            P("user", None, None),
            P("user", "item", None, None),
            P("user", None),
            P("user", "item", None),
            P("user", "item", None, None, None),
            P("user", "item", None),
            P("user", "item", None),
            P("user", "item"),
            P("user", "item", None),
            P("user", "item", None),
            P("user", "item", None),
        ),
        out_specs=(P("user", None, None), P("user", "item", None, None)),
        check_vma=False,
    )
```

```python
import jax
import jax.numpy as jnp
from jax import lax
from jax.experimental import pallas as pl
from jax.experimental.pallas import tpu as pltpu
from jax.sharding import PartitionSpec as P

F32 = jnp.float32
BF16 = jnp.bfloat16
MESH = pl.DeviceIdType.MESH
SIDE = 4
BLOCK = 128
CHUNK = SIDE * BLOCK
HALF = SIDE * CHUNK
ROUNDS = 5
GROUPS = 8


def place(block):
    core = block & 1
    x = (block >> 1) & (SIDE - 1)
    y = block >> 3
    return core * SIDE * SIDE + (y + core * (x - y)) * SIDE + x + core * (y - x)


def build_kernel(
    count_hbm, rows_hbm, cols_hbm, tiles_hbm, r_ref, count_ref, rows_ref, cols_ref, tiles, sems
):
    slots = tiles.shape[0]
    scalars = [
        pltpu.make_async_copy(src, dst, sems.at[GROUPS + i])
        for i, (src, dst) in enumerate(
            ((count_hbm, count_ref), (rows_hbm, rows_ref), (cols_hbm, cols_ref))
        )
    ]
    for item in scalars:
        item.start()
    size = slots // GROUPS
    copies = [
        pltpu.make_async_copy(
            tiles_hbm.at[pl.ds(g * size, size)], tiles.at[pl.ds(g * size, size)], sems.at[g]
        )
        for g in range(GROUPS)
    ]
    for item in copies:
        item.start()
    step = 64

    def clear(i, carry):
        at = pl.ds(pl.multiple_of(i * step, step), step)
        for half in range(2):
            r_ref[half, at, :] = jnp.zeros((step, r_ref.shape[2]), BF16)
        return carry

    lax.fori_loop(0, r_ref.shape[1] // step, clear, 0)

    def add(slot, carry):
        spot = place(cols_ref[0, slot])
        half = spot // (SIDE * SIDE)
        users = pl.ds(pl.multiple_of(rows_ref[0, slot] * BLOCK, BLOCK), BLOCK)
        items = pl.ds(pl.multiple_of((spot % (SIDE * SIDE)) * BLOCK, BLOCK), BLOCK)
        tile = tiles[slot].astype(F32)
        r_ref[half, users, items] = (r_ref[half, users, items].astype(F32) + tile).astype(BF16)
        return carry

    for item in scalars:
        item.wait()
    count = count_ref[0, 0]
    for g in range(GROUPS):
        copies[g].wait()
        lax.fori_loop(g * size, jnp.clip(count, g * size, (g + 1) * size), add, 0)


def build(count, rows, cols, tiles, users):
    hbm = pl.BlockSpec(memory_space=pl.ANY)
    return pl.pallas_call(
        build_kernel,
        out_shape=jax.ShapeDtypeStruct((2, users, HALF), BF16),
        in_specs=[hbm] * 4,
        out_specs=pl.BlockSpec(memory_space=pltpu.VMEM),
        scratch_shapes=[
            pltpu.SMEM(count.shape, jnp.int32),
            pltpu.SMEM(rows.shape, jnp.int32),
            pltpu.SMEM(cols.shape, jnp.int32),
            pltpu.VMEM(tiles.shape, jnp.int32),
            pltpu.SemaphoreType.DMA((GROUPS + 3,)),
        ],
        compiler_params=pltpu.CompilerParams(vmem_limit_bytes=16 * 2**20),
        name="build",
    )(count, rows, cols, tiles)


def over_rows(left, right):
    return lax.dot_general(left, right, (((0,), (0,)), ((), ())), preferred_element_type=F32)


def main_kernel(
    user_emb_hbm, item_emb_hbm, user_degree_hbm, item_degree_hbm, triple_user_hbm,
    triple_pos_hbm, triple_neg_hbm, r_mat,
    out_user, out_item,
    user_emb, item_emb, user_degree, item_degree, triple_user, triple_pos, triple_neg,
    feeds, users, sib_in, sib_out, q_out, q_in, p_out, p_in, z_out, z_in,
    part, upart, user_total, item_total, user_base, item_base, pick_u, pick_i, split, ru, ri,
    load_sem, ag_recv, ag_send, rs_recv, rs_send, z_recv, z_send,
):
    a = lax.axis_index("user")
    z = lax.axis_index("item")
    core = a % 2
    x = (a // 2) % SIDE
    y = a // (2 * SIDE)
    p = x + core * (y - x)
    q = y + core * (x - y)
    rows_u = user_emb.shape[0]
    quarter = rows_u // SIDE
    trips = triple_user.shape[1]
    half_q = quarter // 2

    def at_pq(pp, qq):
        yy = qq + core * (pp - qq)
        xx = pp + core * (qq - pp)
        return {"user": (yy * SIDE + xx) * 2 + core}

    def turn(i, by):
        return (i + by) % SIDE

    to_p = {by: at_pq(turn(p, by), q) for by in (1, 2, 3)}
    to_q = {by: at_pq(p, turn(q, by)) for by in (1, 2, 3)}
    to_z = {by: {"item": turn(z, by)} for by in (1, 2, 3)}
    to_s = {"user": a + 1 - 2 * core}

    def rows(start, count):
        return pl.ds(pl.multiple_of(start, BLOCK), count)

    def copy(src, dst, send, recv, device):
        return pltpu.make_async_remote_copy(
            src_ref=src, dst_ref=dst, send_sem=send, recv_sem=recv,
            device_id=device, device_id_type=MESH,
        )

    loads = [
        pltpu.make_async_copy(src, dst, load_sem.at[i])
        for i, (src, dst) in enumerate((
            (item_degree_hbm, item_degree), (item_emb_hbm, item_emb),
            (user_degree_hbm, user_degree), (user_emb_hbm, user_emb),
            (triple_user_hbm, triple_user), (triple_pos_hbm, triple_pos),
            (triple_neg_hbm, triple_neg),
        ))
    ]
    for load in loads:
        load.start()
    barrier = pltpu.get_barrier_semaphore()
    partners = [*to_p.values(), *to_q.values(), *to_z.values(), to_s]
    for device in partners:
        pl.semaphore_signal(barrier, inc=1, device_id=device, device_id_type=MESH)

    def slot(qq, pp):
        return ((core * SIDE + qq) * SIDE + pp) * BLOCK

    def gather_copy(r, start, count, device, recv):
        ref = feeds.at[r, rows(start, count)]
        return copy(ref, ref, ag_send.at[r], ag_recv.at[r, recv], device)

    def to_sibling(r, qq, pp):
        gather_copy(r, slot(qq, pp), BLOCK, to_s, 15 + qq).start()

    def spread_block(r, rel):
        pp = turn(p, rel)
        for by in (2, 1, 3):
            gather_copy(r, slot(q, pp), BLOCK, to_q[by], 3 + (by - 1) * SIDE + rel).start()
        to_sibling(r, q, pp)

    def gather_start(r):
        for by in (2, 1, 3):
            gather_copy(r, slot(q, p), BLOCK, to_p[by], by - 1).start()
        spread_block(r, 0)

    def gather_p(r):
        for by in (1, 3, 2):
            back = turn(p, SIDE - by)
            gather_copy(r, slot(q, back), BLOCK, to_p[by], by - 1).wait_recv()
            spread_block(r, SIDE - by)

    def gather_q(r, hook=None):
        for rel in (0, 3, 1, 2):
            if rel == 1 and hook is not None:
                hook()
            pp = turn(p, rel)
            for by in (1, 3, 2):
                qq = turn(q, SIDE - by)
                gather_copy(
                    r, slot(qq, pp), BLOCK, to_q[by], 3 + (by - 1) * SIDE + rel
                ).wait_recv()
                to_sibling(r, qq, pp)

    def gather_end(r):
        for other in range(SIDE):
            start = ((1 - core) * SIDE + other) * CHUNK
            gather_copy(r, start, CHUNK, to_s, 15 + other).wait_recv()

    def gather_sent(r):
        gather_copy(r, 0, 31 * BLOCK, to_s, 0).wait_send()

    def feed_half(r, half):
        return feeds[r, rows(half * HALF, HALF), :]

    def sibling_part(r, term, rel):
        theirs = turn(p, rel)
        sib_out[theirs] = term(1 - core, theirs).astype(BF16)
        sibling_copy(r, theirs).start()

    def sibling_copy(r, chunk):
        return copy(
            sib_out.at[chunk], sib_in.at[r, chunk], rs_send.at[r, 0], rs_recv.at[r, chunk], to_s
        )

    def q_copy(r, by, rel):
        at = rows(turn(p, rel) * BLOCK, BLOCK)
        return copy(
            q_out.at[by - 1, at], q_in.at[r, by - 1, at], rs_send.at[r, 1],
            rs_recv.at[r, 4 + (by - 1) * SIDE + rel], to_q[by],
        )

    def p_copy(r, by):
        return copy(
            p_out.at[by - 1], p_in.at[r, by - 1], rs_send.at[r, 2],
            rs_recv.at[r, 15 + by], to_p[by],
        )

    def own_part(r, term, by):
        chunk = turn(q, by)
        part[...] = term(core, chunk)
        sibling_copy(r, chunk).wait_recv()
        value = part[...] + sib_in[r, chunk].astype(F32)
        if by == 0:
            part[...] = value
        else:
            q_out[by - 1] = value.astype(BF16)

    def q_send(r, bys, rels):
        for rel in rels:
            for by in bys:
                q_copy(r, by, rel).start()

    def sum_make(r, term):
        sibling_part(r, term, 2)
        for by, later in ((2, 1), (1, 3), (3, 0)):
            sibling_part(r, term, later)
            own_part(r, term, by)
            q_send(r, (by,), (2, 1, 3))
        q_send(r, (2, 1, 3), (0,))
        own_part(r, term, 0)

    def sum_q(r, rel):
        at = rows(turn(p, rel) * BLOCK, BLOCK)
        value = part[at, :]
        for by in (1, 3, 2):
            q_copy(r, by, rel).wait_recv()
            value = value + q_in[r, by - 1, at, :].astype(F32)
        return value

    def sum_p(r):
        for by in (2, 1, 3):
            p_out[by - 1] = sum_q(r, by).astype(BF16)
            p_copy(r, by).start()

    def sum_end(r):
        value = sum_q(r, 0)
        for by in (1, 3, 2):
            p_copy(r, by).wait_recv()
            value = value + p_in[r, by - 1].astype(F32)
        return value

    def sums_sent(r):
        copy(sib_out, sib_in.at[r], rs_send.at[r, 0], rs_recv.at[r, 0], to_s).wait_send()
        copy(q_out, q_in.at[r], rs_send.at[r, 1], rs_recv.at[r, 4], to_q[1]).wait_send()
        copy(p_out, p_in.at[r], rs_send.at[r, 2], rs_recv.at[r, 16], to_p[1]).wait_send()

    def z_copy(r, by, sub):
        at = rows(sub * half_q, half_q)
        return copy(
            z_out.at[by - 1, at], z_in.at[r, by - 1, at], z_send.at[r, 0],
            z_recv.at[r, (by - 1) * 2 + sub], to_z[by],
        )

    def u_copy(r, owner, by, sub):
        ref = users.at[r + 1, rows(owner * quarter + sub * half_q, half_q)]
        return copy(ref, ref, z_send.at[r, 1], z_recv.at[r, 4 + by * 2 + sub], to_z[by])

    def users_make(r, term):
        for by in (2, 1, 3):
            z_out[by - 1] = term(turn(z, by)).astype(BF16)
            z_copy(r, by, 0).start()
        for by in (2, 1, 3):
            z_copy(r, by, 1).start()
        upart[rows(z * quarter, quarter), :] = term(z)

    def user_turn(r, sub, update):
        at = rows(z * quarter + sub * half_q, half_q)
        own = slice(sub * half_q, (sub + 1) * half_q)
        value = upart[at, :]
        for by in (1, 3, 2):
            z_copy(r, by, sub).wait_recv()
            value = value + z_in[r, by - 1, own, :].astype(F32)
        users[r + 1, at, :] = update(r, own, wide(ru[at, :]), value).astype(BF16)
        for by in (2, 1, 3):
            u_copy(r, z, by, sub).start()

    def user_ready(r):
        for sub in range(2):
            for by in (1, 3, 2):
                u_copy(r, turn(z, SIDE - by), by, sub).wait_recv()

    def z_sent(r):
        copy(z_out, z_in.at[r], z_send.at[r, 0], z_recv.at[r, 0], to_z[1]).wait_send()

    def u_sent(r):
        ref = users.at[r + 1, pl.ds(0, 3 * quarter)]
        copy(ref, ref, z_send.at[r, 1], z_recv.at[r, 6], to_z[1]).wait_send()

    def item_term(r):
        def term(half, chunk):
            return over_rows(r_mat[half, :, rows(chunk * CHUNK, CHUNK)], users[r])

        return term

    def users_first(r):
        def step(i, carry):
            at = rows(i * CHUNK, CHUNK)
            upart[at, :] = jnp.dot(
                r_mat[core, at, :], feed_half(r, core), preferred_element_type=F32
            )
            return carry

        lax.fori_loop(0, rows_u // CHUNK, step, 0)

    def user_term(r):
        def term(owner):
            at = rows(owner * quarter, quarter)
            return upart[at, :] + jnp.dot(
                r_mat[1 - core, at, :], feed_half(r, 1 - core), preferred_element_type=F32
            )

        return term

    def column(line):
        return jnp.broadcast_to(line, (BLOCK, BLOCK)).T

    def wide(scale):
        return jnp.concatenate([scale, scale], axis=1)

    own_u = rows(z * quarter, quarter)
    own_slot = rows(slot(q, p), BLOCK)

    def ri_own():
        return wide(ri[...])

    for load in loads[:2]:
        load.wait()
    ri[...] = column(lax.rsqrt(item_degree[...].astype(F32)))
    ei = item_emb[...].astype(F32)
    feeds[0, own_slot, :] = (ri_own() * ei).astype(BF16)
    pl.semaphore_wait(barrier, len(partners))
    gather_start(0)
    item_total[...] = ei
    for load in loads[2:]:
        load.wait()
    for i in range(rows_u // BLOCK):
        at = slice(i * BLOCK, (i + 1) * BLOCK)
        scale = column(lax.rsqrt(user_degree[:, at].astype(F32)))
        ru[at, :] = scale
        users[0, at, :] = (wide(scale) * user_emb[at, :].astype(F32)).astype(BF16)
    user_total[...] = user_emb[own_u, :].astype(F32)

    def make_picks():
        def spot(ref):
            value = ref[...]
            return place(value >> 7) * BLOCK + (value & (BLOCK - 1))

        def columns(line):
            line = line.astype(F32)
            return jnp.concatenate(
                [column(line[:, i : i + BLOCK]) for i in range(0, trips, BLOCK)], axis=0
            )

        lane = lax.broadcasted_iota(jnp.int32, (trips, BLOCK), 1).astype(F32)
        chosen = columns(triple_user[...])
        for i in range(rows_u // BLOCK):
            hot = (chosen - i * BLOCK == lane).astype(F32)
            pick_u[:, i * BLOCK : (i + 1) * BLOCK] = hot.astype(BF16)
        pos = columns(spot(triple_pos))
        neg = columns(spot(triple_neg))
        for half in range(2):
            for i in range(HALF // BLOCK):
                at = half * HALF + i * BLOCK
                hot = (pos - at == lane).astype(F32) - (neg - at == lane).astype(F32)
                pick_i[half, :, i * BLOCK : (i + 1) * BLOCK] = hot.astype(BF16)

    def users_last(r):
        gather_end(r)
        if r > 0:
            z_sent(r - 1)
        users_make(r, user_term(r))

    def forward_user(r, own, scale, value):
        state = (scale * value).astype(BF16).astype(F32)
        user_total[own, :] += state
        return scale * state if r == 0 else user_total[own, :] / 3.0

    def forward_item(r, value):
        state = (ri_own() * value).astype(BF16).astype(F32)
        item_total[...] += state
        feed = ri_own() * state if r == 0 else item_total[...] / 3.0
        feeds[r + 1, own_slot, :] = feed.astype(BF16)
        gather_start(r + 1)

    term = item_term(0)
    for by in (2, 1, 3, 0):
        sibling_part(0, term, by)
    gather_p(0)
    for by in (2, 1, 3, 0):
        own_part(0, term, by)
    gather_q(0, lambda: q_send(0, (2, 1, 3), (2, 1, 3, 0)))
    users_first(0)
    users_last(0)
    sum_p(0)
    forward_item(0, sum_end(0))
    user_turn(0, 0, forward_user)
    user_turn(0, 1, forward_user)
    make_picks()
    gather_p(1)
    sums_sent(0)
    user_ready(0)
    sum_make(1, item_term(1))
    gather_q(1)
    users_first(1)
    sum_p(1)
    users_last(1)
    forward_item(1, sum_end(1))
    user_turn(1, 0, forward_user)
    user_turn(1, 1, forward_user)

    gather_p(2)
    gather_q(2)
    user_ready(1)
    upart[:trips, :] = jnp.dot(pick_u[...], users[2], preferred_element_type=F32)
    upart[trips : 2 * trips, :] = jnp.dot(
        pick_i[core], feed_half(2, core), preferred_element_type=F32
    )
    gather_end(2)
    diff = upart[trips : 2 * trips, :] + jnp.dot(
        pick_i[1 - core], feed_half(2, 1 - core), preferred_element_type=F32
    )
    user_rows = upart[:trips, :]
    score = jnp.sum(user_rows * diff, axis=1, keepdims=True)
    weight = -jax.nn.sigmoid(-score)
    for i, value in enumerate((weight * diff, weight * user_rows)):
        high = value.astype(BF16)
        split[i, :, :256] = high
        split[i, :, 256:] = (value - high.astype(F32)).astype(BF16)

    def both(product):
        return product[:, :256] + product[:, 256:]

    def grad_user_term(owner):
        return both(over_rows(pick_u[:, rows(owner * quarter, quarter)], split[0]))

    def grad_item_term(half, chunk):
        return both(over_rows(pick_i[half, :, rows(chunk * CHUNK, CHUNK)], split[1]))

    def grad_user(r, own, scale, value):
        user_base[own, :] = value
        return scale * value

    z_sent(1)
    users_make(2, grad_user_term)
    sums_sent(1)
    sum_make(2, grad_item_term)
    user_turn(2, 0, grad_user)
    user_turn(2, 1, grad_user)
    sum_p(2)
    value = sum_end(2)
    item_base[...] = value
    feeds[3, own_slot, :] = (ri_own() * value).astype(BF16)
    gather_start(3)

    def backward_user(r, own, scale, value):
        state = user_base[own, :] + scale * value
        return scale * state if r == 3 else state / 3.0

    sums_sent(2)
    user_ready(2)
    sum_make(3, item_term(3))
    gather_p(3)
    gather_q(3, lambda: sum_p(3))
    state = item_base[...] + ri_own() * sum_end(3)
    feeds[4, own_slot, :] = (ri_own() * state).astype(BF16)
    gather_start(4)
    users_first(3)
    users_last(3)
    gather_p(4)
    user_turn(3, 0, backward_user)
    user_turn(3, 1, backward_user)
    gather_q(4)
    users_first(4)
    users_last(4)
    sums_sent(3)
    user_ready(3)
    sum_make(4, item_term(4))
    user_turn(4, 0, backward_user)
    user_turn(4, 1, backward_user)
    sum_p(4)
    out_item[...] = item_base[...] + ri_own() * sum_end(4)
    user_ready(4)
    out_user[...] = users[5]
    sums_sent(4)
    z_sent(4)
    for r in range(ROUNDS):
        u_sent(r)
        gather_sent(r)


def main(user_emb, item_emb, user_degree, item_degree, triples, r_mat):
    rows_u, width = user_emb.shape
    col_rows = 2 * HALF
    quarter = rows_u // SIDE
    trips = triples[0].shape[1]
    vmem = pl.BlockSpec(memory_space=pltpu.VMEM)
    dma = pltpu.SemaphoreType.DMA
    small = (user_emb, item_emb, user_degree, item_degree, *triples)
    scratch = [pltpu.VMEM(v.shape, v.dtype) for v in small] + [
        pltpu.VMEM((ROUNDS, col_rows, width), BF16),
        pltpu.VMEM((ROUNDS + 1, rows_u, width), BF16),
        pltpu.VMEM((ROUNDS, SIDE, CHUNK, width), BF16),
        pltpu.VMEM((SIDE, CHUNK, width), BF16),
        pltpu.VMEM((3, CHUNK, width), BF16),
        pltpu.VMEM((ROUNDS, 3, CHUNK, width), BF16),
        pltpu.VMEM((3, BLOCK, width), BF16),
        pltpu.VMEM((ROUNDS, 3, BLOCK, width), BF16),
        pltpu.VMEM((3, quarter, width), BF16),
        pltpu.VMEM((ROUNDS, 3, quarter, width), BF16),
        pltpu.VMEM((CHUNK, width), F32),
        pltpu.VMEM((rows_u, width), F32),
        pltpu.VMEM((quarter, width), F32),
        pltpu.VMEM((BLOCK, width), F32),
        pltpu.VMEM((quarter, width), F32),
        pltpu.VMEM((BLOCK, width), F32),
        pltpu.VMEM((trips, rows_u), BF16),
        pltpu.VMEM((2, trips, HALF), BF16),
        pltpu.VMEM((2, trips, 2 * width), BF16),
        pltpu.VMEM((rows_u, BLOCK), F32),
        pltpu.VMEM((BLOCK, BLOCK), F32),
        dma((7,)),
        dma((ROUNDS, 19)),
        dma((ROUNDS,)),
        dma((ROUNDS, 19)),
        dma((ROUNDS, 3)),
        dma((ROUNDS, 12)),
        dma((ROUNDS, 2)),
    ]
    return pl.pallas_call(
        main_kernel,
        out_shape=(
            jax.ShapeDtypeStruct((rows_u, width), BF16),
            jax.ShapeDtypeStruct((BLOCK, width), F32),
        ),
        in_specs=[pl.BlockSpec(memory_space=pl.ANY)] * 7 + [vmem],
        out_specs=(vmem, vmem),
        scratch_shapes=scratch,
        compiler_params=pltpu.CompilerParams(
            collective_id=0, has_side_effects=True, vmem_limit_bytes=44 * 2**20
        ),
        name="propagate",
    )(*small, r_mat)


def per_device(
    user_emb, item_emb, user_degree, item_degree, tiles, tile_user, tile_item, tile_count,
    triple_user, triple_pos, triple_neg,
):
    r_mat = build(tile_count, tile_user[0], tile_item[0], tiles[0, 0], user_emb.shape[1])
    grad_user, grad_item = main(
        user_emb[0], item_emb[0, 0], user_degree, item_degree[0],
        (triple_user[0], triple_pos[0], triple_neg[0]), r_mat,
    )
    return grad_user.astype(F32)[None], (grad_item / 3.0)[None, None]


def solution(mesh):
    return jax.shard_map(
        per_device,
        mesh=mesh,
        in_specs=(
            P("user", None, None),
            P("user", "item", None, None),
            P("user", None),
            P("user", "item", None),
            P("user", "item", None, None, None),
            P("user", "item", None),
            P("user", "item", None),
            P("user", "item"),
            P("user", "item", None),
            P("user", "item", None),
            P("user", "item", None),
        ),
        out_specs=(P("user", None, None), P("user", "item", None, None)),
        check_vma=False,
    )
```

```python
import jax
import jax.numpy as jnp
from jax import lax
from jax.experimental import pallas as pl
from jax.experimental.pallas import tpu as pltpu
from jax.sharding import PartitionSpec as P

F32 = jnp.float32
BF16 = jnp.bfloat16
MESH = pl.DeviceIdType.MESH
SIDE = 4
BLOCK = 128
CHUNK = SIDE * BLOCK
HALF = SIDE * CHUNK
ROUNDS = 5
GROUPS = 8


def place(block):
    core = block & 1
    x = (block >> 1) & (SIDE - 1)
    y = block >> 3
    return core * SIDE * SIDE + (y + core * (x - y)) * SIDE + x + core * (y - x)


def build_kernel(
    count_hbm, rows_hbm, cols_hbm, tiles_hbm, r_ref, count_ref, rows_ref, cols_ref, tiles, sems
):
    slots = tiles.shape[0]
    scalars = [
        pltpu.make_async_copy(src, dst, sems.at[GROUPS + i])
        for i, (src, dst) in enumerate(
            ((count_hbm, count_ref), (rows_hbm, rows_ref), (cols_hbm, cols_ref))
        )
    ]
    for item in scalars:
        item.start()
    size = slots // GROUPS
    copies = [
        pltpu.make_async_copy(
            tiles_hbm.at[pl.ds(g * size, size)], tiles.at[pl.ds(g * size, size)], sems.at[g]
        )
        for g in range(GROUPS)
    ]
    for item in copies:
        item.start()
    step = 64

    def clear(i, carry):
        at = pl.ds(pl.multiple_of(i * step, step), step)
        for half in range(2):
            r_ref[half, at, :] = jnp.zeros((step, r_ref.shape[2]), BF16)
        return carry

    lax.fori_loop(0, r_ref.shape[1] // step, clear, 0)

    def add(slot, carry):
        spot = place(cols_ref[0, slot])
        half = spot // (SIDE * SIDE)
        users = pl.ds(pl.multiple_of(rows_ref[0, slot] * BLOCK, BLOCK), BLOCK)
        items = pl.ds(pl.multiple_of((spot % (SIDE * SIDE)) * BLOCK, BLOCK), BLOCK)
        tile = tiles[slot].astype(F32)
        r_ref[half, users, items] = (r_ref[half, users, items].astype(F32) + tile).astype(BF16)
        return carry

    for item in scalars:
        item.wait()
    count = count_ref[0, 0]
    for g in range(GROUPS):
        copies[g].wait()
        lax.fori_loop(g * size, jnp.clip(count, g * size, (g + 1) * size), add, 0)


def build(count, rows, cols, tiles, users):
    hbm = pl.BlockSpec(memory_space=pl.ANY)
    return pl.pallas_call(
        build_kernel,
        out_shape=jax.ShapeDtypeStruct((2, users, HALF), BF16),
        in_specs=[hbm] * 4,
        out_specs=pl.BlockSpec(memory_space=pltpu.VMEM),
        scratch_shapes=[
            pltpu.SMEM(count.shape, jnp.int32),
            pltpu.SMEM(rows.shape, jnp.int32),
            pltpu.SMEM(cols.shape, jnp.int32),
            pltpu.VMEM(tiles.shape, jnp.int32),
            pltpu.SemaphoreType.DMA((GROUPS + 3,)),
        ],
        compiler_params=pltpu.CompilerParams(vmem_limit_bytes=16 * 2**20),
        name="build",
    )(count, rows, cols, tiles)


def over_rows(left, right):
    return lax.dot_general(left, right, (((0,), (0,)), ((), ())), preferred_element_type=F32)


def main_kernel(
    user_emb_hbm, item_emb_hbm, user_degree_hbm, item_degree_hbm, triple_user_hbm,
    triple_pos_hbm, triple_neg_hbm, r_mat,
    out_user, out_item,
    user_emb, item_emb, user_degree, item_degree, triple_user, triple_pos, triple_neg,
    feeds, users, sib_in, sib_out, q_out, q_in, p_out, p_in, z_out, z_in,
    part, upart, user_total, item_total, user_base, item_base, pick_u, pick_i, split, ru, ri,
    load_sem, ag_recv, ag_send, rs_recv, rs_send, z_recv, z_send,
):
    a = lax.axis_index("user")
    z = lax.axis_index("item")
    core = a % 2
    x = (a // 2) % SIDE
    y = a // (2 * SIDE)
    p = x + core * (y - x)
    q = y + core * (x - y)
    rows_u = user_emb.shape[0]
    quarter = rows_u // SIDE
    trips = triple_user.shape[1]
    half_q = quarter // 2

    def at_pq(pp, qq):
        yy = qq + core * (pp - qq)
        xx = pp + core * (qq - pp)
        return {"user": (yy * SIDE + xx) * 2 + core}

    def turn(i, by):
        return (i + by) % SIDE

    to_p = {by: at_pq(turn(p, by), q) for by in (1, 2, 3)}
    to_q = {by: at_pq(p, turn(q, by)) for by in (1, 2, 3)}
    to_z = {by: {"item": turn(z, by)} for by in (1, 2, 3)}
    to_s = {"user": a + 1 - 2 * core}

    def rows(start, count):
        return pl.ds(pl.multiple_of(start, BLOCK), count)

    def copy(src, dst, send, recv, device):
        return pltpu.make_async_remote_copy(
            src_ref=src, dst_ref=dst, send_sem=send, recv_sem=recv,
            device_id=device, device_id_type=MESH,
        )

    loads = [
        pltpu.make_async_copy(src, dst, load_sem.at[i])
        for i, (src, dst) in enumerate((
            (item_degree_hbm, item_degree), (item_emb_hbm, item_emb),
            (user_degree_hbm, user_degree), (user_emb_hbm, user_emb),
            (triple_user_hbm, triple_user), (triple_pos_hbm, triple_pos),
            (triple_neg_hbm, triple_neg),
        ))
    ]
    for load in loads:
        load.start()
    barrier = pltpu.get_barrier_semaphore()
    partners = [*to_p.values(), *to_q.values(), *to_z.values(), to_s]
    for device in partners:
        pl.semaphore_signal(barrier, inc=1, device_id=device, device_id_type=MESH)

    def slot(qq, pp):
        return ((core * SIDE + qq) * SIDE + pp) * BLOCK

    def gather_copy(r, start, count, device, recv):
        ref = feeds.at[r, rows(start, count)]
        return copy(ref, ref, ag_send.at[r], ag_recv.at[r, recv], device)

    def to_sibling(r, qq, pp):
        gather_copy(r, slot(qq, pp), BLOCK, to_s, 15 + qq).start()

    def spread_block(r, rel):
        pp = turn(p, rel)
        for by in (2, 1, 3):
            gather_copy(r, slot(q, pp), BLOCK, to_q[by], 3 + (by - 1) * SIDE + rel).start()
        to_sibling(r, q, pp)

    def gather_start(r):
        for by in (2, 1, 3):
            gather_copy(r, slot(q, p), BLOCK, to_p[by], by - 1).start()
        spread_block(r, 0)

    def gather_p(r):
        for by in (1, 3, 2):
            back = turn(p, SIDE - by)
            gather_copy(r, slot(q, back), BLOCK, to_p[by], by - 1).wait_recv()
            spread_block(r, SIDE - by)

    def gather_q(r, hook=None):
        for rel in (0, 3, 1, 2):
            if rel == 1 and hook is not None:
                hook()
            pp = turn(p, rel)
            for by in (1, 3, 2):
                qq = turn(q, SIDE - by)
                gather_copy(
                    r, slot(qq, pp), BLOCK, to_q[by], 3 + (by - 1) * SIDE + rel
                ).wait_recv()
                to_sibling(r, qq, pp)

    def gather_end(r):
        for other in range(SIDE):
            start = ((1 - core) * SIDE + other) * CHUNK
            gather_copy(r, start, CHUNK, to_s, 15 + other).wait_recv()

    def gather_sent(r):
        gather_copy(r, 0, 31 * BLOCK, to_s, 0).wait_send()

    def feed_half(r, half):
        return feeds[r, rows(half * HALF, HALF), :]

    def sibling_part(r, term, rel):
        theirs = turn(p, rel)
        sib_out[theirs] = term(1 - core, theirs).astype(BF16)
        sibling_copy(r, theirs).start()

    def sibling_copy(r, chunk):
        return copy(
            sib_out.at[chunk], sib_in.at[r, chunk], rs_send.at[r, 0], rs_recv.at[r, chunk], to_s
        )

    def q_copy(r, by, rel):
        at = rows(turn(p, rel) * BLOCK, BLOCK)
        return copy(
            q_out.at[by - 1, at], q_in.at[r, by - 1, at], rs_send.at[r, 1],
            rs_recv.at[r, 4 + (by - 1) * SIDE + rel], to_q[by],
        )

    def p_copy(r, by):
        return copy(
            p_out.at[by - 1], p_in.at[r, by - 1], rs_send.at[r, 2],
            rs_recv.at[r, 15 + by], to_p[by],
        )

    def own_part(r, term, by):
        chunk = turn(q, by)
        part[...] = term(core, chunk)
        sibling_copy(r, chunk).wait_recv()
        value = part[...] + sib_in[r, chunk].astype(F32)
        if by == 0:
            part[...] = value
        else:
            q_out[by - 1] = value.astype(BF16)

    def q_send(r, bys, rels):
        for rel in rels:
            for by in bys:
                q_copy(r, by, rel).start()

    def sum_make(r, term):
        sibling_part(r, term, 2)
        for by, later in ((2, 1), (1, 3), (3, 0)):
            sibling_part(r, term, later)
            own_part(r, term, by)
            q_send(r, (by,), (2, 1, 3))
        q_send(r, (2, 1, 3), (0,))
        own_part(r, term, 0)

    def sum_q(r, rel):
        at = rows(turn(p, rel) * BLOCK, BLOCK)
        value = part[at, :]
        for by in (1, 3, 2):
            q_copy(r, by, rel).wait_recv()
            value = value + q_in[r, by - 1, at, :].astype(F32)
        return value

    def sum_p(r):
        for by in (2, 1, 3):
            p_out[by - 1] = sum_q(r, by).astype(BF16)
            p_copy(r, by).start()

    def sum_end(r):
        value = sum_q(r, 0)
        for by in (1, 3, 2):
            p_copy(r, by).wait_recv()
            value = value + p_in[r, by - 1].astype(F32)
        return value

    def sums_sent(r):
        copy(sib_out, sib_in.at[r], rs_send.at[r, 0], rs_recv.at[r, 0], to_s).wait_send()
        copy(q_out, q_in.at[r], rs_send.at[r, 1], rs_recv.at[r, 4], to_q[1]).wait_send()
        copy(p_out, p_in.at[r], rs_send.at[r, 2], rs_recv.at[r, 16], to_p[1]).wait_send()

    def z_copy(r, by, sub):
        at = rows(sub * half_q, half_q)
        return copy(
            z_out.at[by - 1, at], z_in.at[r, by - 1, at], z_send.at[r, 0],
            z_recv.at[r, (by - 1) * 2 + sub], to_z[by],
        )

    def u_copy(r, owner, by, sub):
        ref = users.at[r + 1, rows(owner * quarter + sub * half_q, half_q)]
        return copy(ref, ref, z_send.at[r, 1], z_recv.at[r, 4 + by * 2 + sub], to_z[by])

    def users_make(r, term):
        for by in (2, 1, 3):
            z_out[by - 1] = term(turn(z, by)).astype(BF16)
            z_copy(r, by, 0).start()
        for by in (2, 1, 3):
            z_copy(r, by, 1).start()
        upart[rows(z * quarter, quarter), :] = term(z)

    def user_turn(r, sub, update):
        at = rows(z * quarter + sub * half_q, half_q)
        own = slice(sub * half_q, (sub + 1) * half_q)
        value = upart[at, :]
        for by in (1, 3, 2):
            z_copy(r, by, sub).wait_recv()
            value = value + z_in[r, by - 1, own, :].astype(F32)
        users[r + 1, at, :] = update(r, own, wide(ru[at, :]), value).astype(BF16)
        for by in (2, 1, 3):
            u_copy(r, z, by, sub).start()

    def user_ready(r):
        for sub in range(2):
            for by in (1, 3, 2):
                u_copy(r, turn(z, SIDE - by), by, sub).wait_recv()

    def z_sent(r):
        copy(z_out, z_in.at[r], z_send.at[r, 0], z_recv.at[r, 0], to_z[1]).wait_send()

    def u_sent(r):
        ref = users.at[r + 1, pl.ds(0, 3 * quarter)]
        copy(ref, ref, z_send.at[r, 1], z_recv.at[r, 6], to_z[1]).wait_send()

    def item_term(r):
        def term(half, chunk):
            return over_rows(r_mat[half, :, rows(chunk * CHUNK, CHUNK)], users[r])

        return term

    def users_first(r):
        def step(i, carry):
            at = rows(i * CHUNK, CHUNK)
            upart[at, :] = jnp.dot(
                r_mat[core, at, :], feed_half(r, core), preferred_element_type=F32
            )
            return carry

        lax.fori_loop(0, rows_u // CHUNK, step, 0)

    def user_term(r):
        def term(owner):
            at = rows(owner * quarter, quarter)
            return upart[at, :] + jnp.dot(
                r_mat[1 - core, at, :], feed_half(r, 1 - core), preferred_element_type=F32
            )

        return term

    def column(line):
        return jnp.broadcast_to(line, (BLOCK, BLOCK)).T

    def wide(scale):
        return jnp.concatenate([scale, scale], axis=1)

    own_u = rows(z * quarter, quarter)
    own_slot = rows(slot(q, p), BLOCK)

    def ri_own():
        return wide(ri[...])

    for load in loads[:2]:
        load.wait()
    ri[...] = column(lax.rsqrt(item_degree[...].astype(F32)))
    ei = item_emb[...].astype(F32)
    feeds[0, own_slot, :] = (ri_own() * ei).astype(BF16)
    pl.semaphore_wait(barrier, len(partners))
    gather_start(0)
    item_total[...] = ei
    for load in loads[2:]:
        load.wait()
    for i in range(rows_u // BLOCK):
        at = slice(i * BLOCK, (i + 1) * BLOCK)
        scale = column(lax.rsqrt(user_degree[:, at].astype(F32)))
        ru[at, :] = scale
        users[0, at, :] = (wide(scale) * user_emb[at, :].astype(F32)).astype(BF16)
    user_total[...] = user_emb[own_u, :].astype(F32)

    def make_picks():
        def spot(ref):
            value = ref[...]
            return place(value >> 7) * BLOCK + (value & (BLOCK - 1))

        def columns(line):
            line = line.astype(F32)
            return jnp.concatenate(
                [column(line[:, i : i + BLOCK]) for i in range(0, trips, BLOCK)], axis=0
            )

        lane = lax.broadcasted_iota(jnp.int32, (trips, BLOCK), 1).astype(F32)
        chosen = columns(triple_user[...])
        for i in range(rows_u // BLOCK):
            hot = (chosen - i * BLOCK == lane).astype(F32)
            pick_u[:, i * BLOCK : (i + 1) * BLOCK] = hot.astype(BF16)
        pos = columns(spot(triple_pos))
        neg = columns(spot(triple_neg))
        for half in range(2):
            for i in range(HALF // BLOCK):
                at = half * HALF + i * BLOCK
                hot = (pos - at == lane).astype(F32) - (neg - at == lane).astype(F32)
                pick_i[half, :, i * BLOCK : (i + 1) * BLOCK] = hot.astype(BF16)

    def users_last(r):
        gather_end(r)
        if r > 0:
            z_sent(r - 1)
        users_make(r, user_term(r))

    def forward_user(r, own, scale, value):
        state = (scale * value).astype(BF16).astype(F32)
        user_total[own, :] += state
        return scale * state if r == 0 else user_total[own, :] / 3.0

    def forward_item(r, value):
        state = (ri_own() * value).astype(BF16).astype(F32)
        item_total[...] += state
        feed = ri_own() * state if r == 0 else item_total[...] / 3.0
        feeds[r + 1, own_slot, :] = feed.astype(BF16)
        gather_start(r + 1)

    term = item_term(0)
    for by in (2, 1, 3, 0):
        sibling_part(0, term, by)
    gather_p(0)
    for by in (2, 1, 3, 0):
        own_part(0, term, by)
    gather_q(0, lambda: q_send(0, (2, 1, 3), (2, 1, 3, 0)))
    users_first(0)
    users_last(0)
    sum_p(0)
    forward_item(0, sum_end(0))
    user_turn(0, 0, forward_user)
    user_turn(0, 1, forward_user)
    make_picks()
    gather_p(1)
    sums_sent(0)
    user_ready(0)
    sum_make(1, item_term(1))
    gather_q(1)
    users_first(1)
    users_last(1)
    sum_p(1)
    forward_item(1, sum_end(1))
    user_turn(1, 0, forward_user)
    user_turn(1, 1, forward_user)

    gather_p(2)
    gather_q(2)
    user_ready(1)
    upart[:trips, :] = jnp.dot(pick_u[...], users[2], preferred_element_type=F32)
    upart[trips : 2 * trips, :] = jnp.dot(
        pick_i[core], feed_half(2, core), preferred_element_type=F32
    )
    gather_end(2)
    diff = upart[trips : 2 * trips, :] + jnp.dot(
        pick_i[1 - core], feed_half(2, 1 - core), preferred_element_type=F32
    )
    user_rows = upart[:trips, :]
    score = jnp.sum(user_rows * diff, axis=1, keepdims=True)
    weight = -jax.nn.sigmoid(-score)
    for i, value in enumerate((weight * diff, weight * user_rows)):
        high = value.astype(BF16)
        split[i, :, :256] = high
        split[i, :, 256:] = (value - high.astype(F32)).astype(BF16)

    def both(product):
        return product[:, :256] + product[:, 256:]

    def grad_user_term(owner):
        return both(over_rows(pick_u[:, rows(owner * quarter, quarter)], split[0]))

    def grad_item_term(half, chunk):
        return both(over_rows(pick_i[half, :, rows(chunk * CHUNK, CHUNK)], split[1]))

    def grad_user(r, own, scale, value):
        user_base[own, :] = value
        return scale * value

    z_sent(1)
    users_make(2, grad_user_term)
    sums_sent(1)
    sum_make(2, grad_item_term)
    user_turn(2, 0, grad_user)
    user_turn(2, 1, grad_user)
    sum_p(2)
    value = sum_end(2)
    item_base[...] = value
    feeds[3, own_slot, :] = (ri_own() * value).astype(BF16)
    gather_start(3)

    def backward_user(r, own, scale, value):
        state = user_base[own, :] + scale * value
        return scale * state if r == 3 else state / 3.0

    sums_sent(2)
    user_ready(2)
    sum_make(3, item_term(3))
    gather_p(3)
    gather_q(3, lambda: sum_p(3))
    state = item_base[...] + ri_own() * sum_end(3)
    feeds[4, own_slot, :] = (ri_own() * state).astype(BF16)
    gather_start(4)
    users_first(3)
    users_last(3)
    gather_p(4)
    user_turn(3, 0, backward_user)
    user_turn(3, 1, backward_user)
    gather_q(4)
    users_first(4)
    users_last(4)
    sums_sent(3)
    user_ready(3)
    sum_make(4, item_term(4))
    user_turn(4, 0, backward_user)
    user_turn(4, 1, backward_user)
    sum_p(4)
    out_item[...] = item_base[...] + ri_own() * sum_end(4)
    user_ready(4)
    out_user[...] = users[5]
    sums_sent(4)
    z_sent(4)
    for r in range(ROUNDS):
        u_sent(r)
        gather_sent(r)


def main(user_emb, item_emb, user_degree, item_degree, triples, r_mat):
    rows_u, width = user_emb.shape
    col_rows = 2 * HALF
    quarter = rows_u // SIDE
    trips = triples[0].shape[1]
    vmem = pl.BlockSpec(memory_space=pltpu.VMEM)
    dma = pltpu.SemaphoreType.DMA
    small = (user_emb, item_emb, user_degree, item_degree, *triples)
    scratch = [pltpu.VMEM(v.shape, v.dtype) for v in small] + [
        pltpu.VMEM((ROUNDS, col_rows, width), BF16),
        pltpu.VMEM((ROUNDS + 1, rows_u, width), BF16),
        pltpu.VMEM((ROUNDS, SIDE, CHUNK, width), BF16),
        pltpu.VMEM((SIDE, CHUNK, width), BF16),
        pltpu.VMEM((3, CHUNK, width), BF16),
        pltpu.VMEM((ROUNDS, 3, CHUNK, width), BF16),
        pltpu.VMEM((3, BLOCK, width), BF16),
        pltpu.VMEM((ROUNDS, 3, BLOCK, width), BF16),
        pltpu.VMEM((3, quarter, width), BF16),
        pltpu.VMEM((ROUNDS, 3, quarter, width), BF16),
        pltpu.VMEM((CHUNK, width), F32),
        pltpu.VMEM((rows_u, width), F32),
        pltpu.VMEM((quarter, width), F32),
        pltpu.VMEM((BLOCK, width), F32),
        pltpu.VMEM((quarter, width), F32),
        pltpu.VMEM((BLOCK, width), F32),
        pltpu.VMEM((trips, rows_u), BF16),
        pltpu.VMEM((2, trips, HALF), BF16),
        pltpu.VMEM((2, trips, 2 * width), BF16),
        pltpu.VMEM((rows_u, BLOCK), F32),
        pltpu.VMEM((BLOCK, BLOCK), F32),
        dma((7,)),
        dma((ROUNDS, 19)),
        dma((ROUNDS,)),
        dma((ROUNDS, 19)),
        dma((ROUNDS, 3)),
        dma((ROUNDS, 12)),
        dma((ROUNDS, 2)),
    ]
    return pl.pallas_call(
        main_kernel,
        out_shape=(
            jax.ShapeDtypeStruct((rows_u, width), BF16),
            jax.ShapeDtypeStruct((BLOCK, width), F32),
        ),
        in_specs=[pl.BlockSpec(memory_space=pl.ANY)] * 7 + [vmem],
        out_specs=(vmem, vmem),
        scratch_shapes=scratch,
        compiler_params=pltpu.CompilerParams(
            collective_id=0, has_side_effects=True, vmem_limit_bytes=44 * 2**20
        ),
        name="propagate",
    )(*small, r_mat)


def per_device(
    user_emb, item_emb, user_degree, item_degree, tiles, tile_user, tile_item, tile_count,
    triple_user, triple_pos, triple_neg,
):
    r_mat = build(tile_count, tile_user[0], tile_item[0], tiles[0, 0], user_emb.shape[1])
    grad_user, grad_item = main(
        user_emb[0], item_emb[0, 0], user_degree, item_degree[0],
        (triple_user[0], triple_pos[0], triple_neg[0]), r_mat,
    )
    return grad_user.astype(F32)[None], (grad_item / 3.0)[None, None]


def solution(mesh):
    return jax.shard_map(
        per_device,
        mesh=mesh,
        in_specs=(
            P("user", None, None),
            P("user", "item", None, None),
            P("user", None),
            P("user", "item", None),
            P("user", "item", None, None, None),
            P("user", "item", None),
            P("user", "item", None),
            P("user", "item"),
            P("user", "item", None),
            P("user", "item", None),
            P("user", "item", None),
        ),
        out_specs=(P("user", None, None), P("user", "item", None, None)),
        check_vma=False,
    )
```
